128 devices in a mesh: range: 8 (over y, core), chan: 16 (over x, z).
Axes of the slice: x: 4, y: 4, z: 4, core: 2. Of those that a mesh axis runs over, the one named last changes fastest.
Arguments:
- echoes: float32 [2, 64, 512, 2048], P(None, 'chan', None, 'range'), may hold values from -18 to 18
- chirp: float32 [2, 129], replicated, may hold values from -0.375 to 0.375
- train_mask: int32 [512, 16], P('chan', 'range'), may hold values from 0 to 1, as said below
Outputs:
- spectra: bfloat16 [2, 512, 64, 2048], P(None, 'chan', None, 'range')
- factors: float32 [512, 2, 128, 128], P('chan')
The draws below stay inside these ranges and needn't reach their ends.
Inputs may be any that keep to these rules, and one draw needn't show every extreme that they name: `train_mask`: in each Doppler bin exactly 4 consecutive tiles are 0 and all other tiles are 1.
All inputs are finite; a program needn't handle non-finite values.
Results may differ from the reference program's by a relative error of at most 0.001.
Values sent between devices are 32-bit elements; how exact they have to be, the bound alone decides.
No kernel may reach another device: no remote copies, remote signals or barrier semaphores. Data moves between devices by JAX's collectives and lax.ppermute only.
A program may use at most 128 MiB of HBM per device.

```python
import math
import jax
import jax.numpy as jnp
from jax import lax

CH = 64
PULSES = 512
TAPS = 129
TILE = 128
EXCL = 4
GATES = 2048
NTILES = 16


def draw_echoes(key, part):
    noise_key, level_key = jax.random.split(key)
    levels = jnp.exp(jax.random.uniform(level_key, (NTILES,), jnp.float32, math.log(0.3), math.log(3.0)))
    noise_draw = jnp.clip(jax.random.normal(noise_key, (2, CH, PULSES, GATES), jnp.float32), -6.0, 6.0)
    profile = jnp.broadcast_to(levels[:, None], (NTILES, TILE)).reshape(GATES)
    return noise_draw * profile


def draw_train_mask(key, part):
    starts = jax.random.randint(key, (PULSES, 1), 0, NTILES - EXCL + 1)
    tile_index = jnp.arange(NTILES, dtype=jnp.int32)[None, :]
    inside = (tile_index >= starts) & (tile_index < starts + EXCL)
    return jnp.where(inside, 0, 1).astype(jnp.int32)


def centred(key, extent, spread, reach, held_as=jnp.bfloat16):
    array = jax.random.normal(key, extent, jnp.float32) * spread
    return jnp.minimum(jnp.maximum(array, -reach), reach).astype(held_as)


def setup_inputs(seed: int = 0) -> dict:
    splits = jax.random.split(jax.random.key(seed), 4)
    echoes = draw_echoes(jax.random.fold_in(splits[3], 71), 0)
    chirp = centred(splits[1], (2, TAPS), (2 * TAPS) ** -0.5, 0.375, jnp.float32)
    train_mask = draw_train_mask(jax.random.fold_in(splits[3], 71), 0)
    return {"echoes": echoes, "chirp": chirp, "train_mask": train_mask}


best_precision = lax.Precision.HIGHEST

def toeplitz_rows(taps):
    tap_span = taps.shape[-1] - 1
    padded = jnp.concatenate([taps, jnp.zeros((taps.shape[0], tap_span), taps.dtype)], -1)
    tiled = jnp.tile(padded, (1, tap_span))
    return tiled[:, :2 * tap_span * tap_span].reshape(taps.shape[0], tap_span, 2 * tap_span)

def compress(extended, taps):
    tap_span = taps.shape[-1] - 1
    lead_shape = extended.shape[:-1]
    block_count = extended.shape[-1] // tap_span - 1
    blocks = extended.reshape(lead_shape + (block_count + 1, tap_span))
    window = jnp.concatenate([blocks[..., :block_count, :], blocks[..., 1:, :]], -1)
    kernel = toeplitz_rows(taps)
    products = jnp.einsum('tcpnk,sok->tscpno', window, kernel, precision=best_precision, preferred_element_type=jnp.float32)
    real_part = products[0, 0] + products[1, 1]
    imag_part = products[1, 0] - products[0, 1]
    return jnp.stack([real_part, imag_part]).reshape(lead_shape + (block_count * tap_span,))

def doppler_table(bin_numbers, pulse_count):
    phase_index = bin_numbers[:, None] * jnp.arange(pulse_count, dtype=jnp.int32)[None, :] % pulse_count
    angles = phase_index.astype(jnp.float32) * (2.0 * math.pi / pulse_count)
    scaling = 1.0 / math.sqrt(pulse_count)
    return jnp.stack([jnp.cos(angles) * scaling, -jnp.sin(angles) * scaling])

def doppler(signal, dft_table):
    products = jnp.einsum('sdp,tcpg->stdcg', dft_table, signal, precision=best_precision, preferred_element_type=jnp.float32)
    return jnp.stack([products[0, 0] - products[1, 1], products[0, 1] + products[1, 0]])

def gram_block(spectra_now, spectra_next, weights, scaling):
    snapshot = jnp.concatenate([spectra_now, spectra_next], 2)
    masked = snapshot * weights[None, :, None, :]
    products = jnp.einsum('tbkg,sblg->btskl', masked, snapshot, precision=best_precision, preferred_element_type=jnp.float32)
    real_part = products[:, 0, 0] + products[:, 1, 1]
    imag_part = products[:, 0, 1] - products[:, 1, 0]
    return jnp.stack([real_part, imag_part], 1) * scaling

def factor(gram):
    order_size = gram.shape[-1]
    strip_size = min(16, order_size)
    columns = jnp.arange(order_size, dtype=jnp.int32)
    remaining = gram
    pieces = []
    for offset in range(0, order_size, strip_size):
        strip_rows = remaining[:, :, :strip_size, :]

        def column_step(position, carry):
            strip_now, found_rows = carry
            place = offset + position
            row_now = lax.dynamic_index_in_dim(strip_now, position, 2, keepdims=False)
            pivots = lax.optimization_barrier(jnp.sum(jnp.where(columns == place, row_now[:, 0], 0.0), -1))
            inverse = lax.rsqrt(pivots)[:, None]
            row_real = jnp.where(columns >= place, row_now[:, 0] * inverse, 0.0)
            row_imag = jnp.where(columns > place, row_now[:, 1] * inverse, 0.0)
            coef_real = row_real[:, offset:offset + strip_size]
            coef_imag = row_imag[:, offset:offset + strip_size]
            new_real = strip_now[:, 0] - coef_real[:, :, None] * row_real[:, None, :] - coef_imag[:, :, None] * row_imag[:, None, :]
            new_imag = strip_now[:, 1] - coef_real[:, :, None] * row_imag[:, None, :] + coef_imag[:, :, None] * row_real[:, None, :]
            found_rows = lax.dynamic_update_index_in_dim(found_rows, jnp.stack([row_real, row_imag], 1), position, 2)
            return (jnp.stack([new_real, new_imag], 1), found_rows)
        strip_end, found_rows = lax.fori_loop(0, strip_size, column_step, (strip_rows, jnp.zeros_like(strip_rows)))
        pieces.append(found_rows)
        if offset + strip_size < order_size:
            tail_part = found_rows[:, :, :, offset + strip_size:]
            products = jnp.einsum('nabi,ncbj->nacij', tail_part, found_rows, precision=best_precision, preferred_element_type=jnp.float32)
            update_real = products[:, 0, 0] + products[:, 1, 1]
            update_imag = products[:, 0, 1] - products[:, 1, 0]
            remaining = remaining[:, :, strip_size:, :] - jnp.stack([update_real, update_imag], 1)
    return jnp.concatenate(pieces, 2)

def reference(echoes, chirp, train_mask):
    tap_span = TAPS - 1
    dft_table = doppler_table(jnp.arange(PULSES, dtype=jnp.int32), PULSES)

    def per_channel(channel_index):
        channel_data = lax.dynamic_index_in_dim(echoes, channel_index, 1, keepdims=False)
        padded = jnp.concatenate([channel_data, jnp.zeros((2, PULSES, tap_span), channel_data.dtype)], -1)
        compressed = compress(padded[:, None], chirp)
        return doppler(compressed, dft_table)[:, :, 0]
    per_chan = lax.map(per_channel, jnp.arange(CH, dtype=jnp.int32))
    spectra_full = jnp.moveaxis(per_chan, 0, 2)
    weights = jnp.broadcast_to(train_mask.astype(jnp.float32)[:, :, None], (PULSES, NTILES, TILE)).reshape(PULSES, GATES)
    scaling = 1.0 / GATES

    def per_bin(bin_index):
        bin_now = lax.dynamic_slice_in_dim(spectra_full, bin_index, 1, 1)
        bin_after = lax.dynamic_slice_in_dim(spectra_full, (bin_index + 1) % PULSES, 1, 1)
        return gram_block(bin_now, bin_after, lax.dynamic_slice_in_dim(weights, bin_index, 1, 0), scaling)[0]
    gram_all = lax.map(per_bin, jnp.arange(PULSES, dtype=jnp.int32))
    factors = factor(gram_all)
    return (spectra_full.astype(jnp.bfloat16), factors)
```

```python
import functools
import math

import jax
import jax.numpy as jnp
import numpy as np
from jax import lax
from jax.experimental import pallas as pl
from jax.experimental.pallas import tpu as pltpu
from jax.sharding import PartitionSpec as P

PULSES = 512
TILE = 128
BINS = 32
WIDE = BINS + 1
CHANS = 16
LOCAL = 4
LATE = 8
EARLY = BINS - LATE
STRIP = 16
F32 = jnp.float32
BF16 = jnp.bfloat16
VMEM = pl.BlockSpec(memory_space=pltpu.VMEM)
SMEM = pl.BlockSpec(memory_space=pltpu.SMEM)
ANY = pl.BlockSpec(memory_space=pl.ANY)


def params(mib=48):
    return pltpu.CompilerParams(vmem_limit_bytes=mib << 20)


def cost(flops, nbytes):
    return pl.CostEstimate(flops=int(flops), bytes_accessed=int(nbytes), transcendentals=0)


def split(value):
    high = value.astype(BF16)
    return high, (value - high.astype(F32)).astype(BF16)


def dot3(left, right, contract=((1,), (0,))):
    lh, ll = left
    rh, rl = right
    dims = (contract, ((), ()))
    dot = functools.partial(lax.dot_general, dimension_numbers=dims, preferred_element_type=F32)
    return dot(lh, rh) + (dot(lh, rl) + dot(ll, rh))


def doppler_matrices():
    rows = np.arange(128)[:, None]
    pulses = np.arange(128)[None, :]
    found = []
    for j in range(4):
        angle = ((4 * rows + j) * pulses % PULSES) * (2.0 * math.pi / PULSES)
        c, s = np.cos(angle), np.sin(angle)
        found.append(np.block([[c, s], [-s, c]]) / math.sqrt(PULSES))
    full = np.stack(found).astype(np.float32)
    high = full.astype(jnp.bfloat16)
    low = (full - high.astype(np.float32)).astype(jnp.bfloat16)
    return np.stack([high, low])


def fill_toeplitz(chirp_ref, pad_ref, kmat_ref):
    pad_ref[...] = jnp.zeros_like(pad_ref)
    pad_ref[0:2, 0 : TILE + 1] = chirp_ref[...]
    taps = []
    for part in range(2):
        row = jnp.broadcast_to(pad_ref[part : part + 1, :], (TILE, 2 * TILE))
        taps.append(pltpu.roll(row, 0, 1, stride=1, stride_axis=0).T)
    re, im = taps
    full = jnp.concatenate(
        [jnp.concatenate([re, -im], 1), jnp.concatenate([im, re], 1)], 0
    )
    kmat_ref[0], kmat_ref[1] = split(full)


def front_body(step, windows, kmat_ref, w_ref, store):
    tables = (kmat_ref[0], kmat_ref[1])
    quarters = [[], [], [], []]
    for window in windows:
        y = dot3(split(window), tables)
        y0, y1, y2, y3 = (y[128 * q : 128 * q + 128] for q in range(4))
        s02, d02, s13, d13 = y0 + y2, y0 - y2, y1 + y3, y1 - y3
        d02r, d02i, d13r, d13i = d02[:, :128], d02[:, 128:], d13[:, :128], d13[:, 128:]
        z0, z2 = s02 + s13, s02 - s13
        quarters[0].append((z0[:, :128], z0[:, 128:]))
        quarters[1].append((d02r + d13i, d02i - d13r))
        quarters[2].append((z2[:, :128], z2[:, 128:]))
        quarters[3].append((d02r - d13i, d02i + d13r))
    for j in range(4):
        (r0, i0), (r1, i1) = quarters[j]
        data = jnp.concatenate(
            [jnp.concatenate([r0, r1], 1), jnp.concatenate([i0, i1], 1)], 0
        )
        out = dot3((w_ref[0, j], w_ref[1, j]), split(data))
        for part in range(2):
            for c in range(2):
                store(j, part, c, out[128 * part : 128 * part + 128, 128 * c : 128 * c + 128])


def store_into(flat_ref, step):
    def store(j, part, c, block):
        for k in range(CHANS):
            start = k * WIDE * 8 + j * 8 + part * 4 + c + 2 * step
            flat_ref[pl.ds(start, 8, stride=32), :] = block[8 * k : 8 * k + 8]

    return store


def add_edges(flat_ref):
    for k in range(CHANS):
        source = ((k + 1) % CHANS) * WIDE * 8
        flat_ref[pl.ds(k * WIDE * 8 + BINS * 8, 8), :] = flat_ref[pl.ds(source, 8), :]


def front0_kernel(chirp_ref, x_ref, w_ref, out_ref, rim_ref, pad_ref, kmat_ref):
    step = pl.program_id(0)

    @pl.when(step == 0)
    def _():
        fill_toeplitz(chirp_ref, pad_ref, kmat_ref)

    windows = []
    for c in range(2):
        windows.append(jnp.concatenate([x_ref[0, c], x_ref[1, c]], 1))
    rim_ref[...] = x_ref[:, :, :, :TILE]
    front_body(step, windows, kmat_ref, w_ref, store_into(out_ref, step))

    @pl.when(step == 1)
    def _():
        add_edges(out_ref)


def front1_kernel(chirp_ref, x_ref, h_ref, w_ref, a_ref, b_ref, pad_ref, kmat_ref, flat_ref):
    step = pl.program_id(0)

    @pl.when(step == 0)
    def _():
        fill_toeplitz(chirp_ref, pad_ref, kmat_ref)

    windows = []
    for c in range(2):
        windows.append(jnp.concatenate([x_ref[0, c], h_ref[0, c], x_ref[1, c], h_ref[1, c]], 1))
    front_body(step, windows, kmat_ref, w_ref, store_into(flat_ref, step))

    @pl.when(step == 1)
    def _():
        add_edges(flat_ref)
        for k in range(CHANS):
            base = k * WIDE * 8
            middle = (EARLY + 1) * 8
            a_ref[k] = flat_ref[pl.ds(base, middle), :]
            b_ref[k] = flat_ref[pl.ds(base + middle, LATE * 8), :]


def front_scratch():
    return [pltpu.VMEM((8, 2 * TILE), F32), pltpu.VMEM((2, 4 * TILE, 2 * TILE), BF16)]


def front0(chirp, echoes, w):
    return pl.pallas_call(
        front0_kernel,
        grid=(2,),
        in_specs=[
            pl.BlockSpec(chirp.shape, lambda i: (0, 0)),
            pl.BlockSpec((2, 2, PULSES, 2 * TILE), lambda i: (0, i, 0, 0)),
            pl.BlockSpec(w.shape, lambda i: (0, 0, 0, 0)),
        ],
        out_specs=[
            pl.BlockSpec((CHANS * WIDE * 8, TILE), lambda i: (0, 0)),
            pl.BlockSpec((2, 2, PULSES, TILE), lambda i: (0, i, 0, 0)),
        ],
        out_shape=[
            jax.ShapeDtypeStruct((CHANS * WIDE * 8, TILE), F32),
            jax.ShapeDtypeStruct((2, LOCAL, PULSES, TILE), F32),
        ],
        scratch_shapes=front_scratch(),
        compiler_params=params(),
        cost_estimate=cost(4e9, 12e6),
        name="front0",
    )(chirp, echoes, w)


def front1(chirp, echoes, rim, w):
    return pl.pallas_call(
        front1_kernel,
        grid=(2,),
        in_specs=[
            pl.BlockSpec(chirp.shape, lambda i: (0, 0)),
            pl.BlockSpec((2, 2, PULSES, TILE), lambda i: (0, i, 0, 1)),
            pl.BlockSpec((2, 2, PULSES, TILE), lambda i: (0, i, 0, 0)),
            pl.BlockSpec(w.shape, lambda i: (0, 0, 0, 0)),
        ],
        out_specs=[
            pl.BlockSpec((CHANS, (EARLY + 1) * 8, TILE), lambda i: (0, 0, 0)),
            pl.BlockSpec((CHANS, LATE * 8, TILE), lambda i: (0, 0, 0)),
        ],
        out_shape=[
            jax.ShapeDtypeStruct((CHANS, (EARLY + 1) * 8, TILE), F32),
            jax.ShapeDtypeStruct((CHANS, LATE * 8, TILE), F32),
        ],
        scratch_shapes=front_scratch() + [pltpu.VMEM((CHANS * WIDE * 8, TILE), F32)],
        compiler_params=params(),
        cost_estimate=cost(4e9, 8e6),
        name="front1",
    )(chirp, echoes, rim, w)


def unweave(blocks):
    pairs = blocks.reshape(CHANS // 2, 2, 8, TILE)
    even, odd = pairs[:, 0], pairs[:, 1]
    first = lax.broadcasted_iota(jnp.int32, even.shape, 1) < 4
    even_turned = pltpu.roll(even, 4, 1)
    odd_turned = pltpu.roll(odd, 4, 1)
    re = jnp.where(first, even, odd_turned).reshape(CHANS * LOCAL, TILE)
    im = jnp.where(first, even_turned, odd).reshape(CHANS * LOCAL, TILE)
    return re, im


def plant(place, blocks, store_spectra, high_ref, low_ref):
    re, im = unweave(blocks)
    rh, rl = split(re)
    ih, il = split(im)
    store_spectra(rh, ih)
    high_ref[0, place] = jnp.concatenate([rh, ih], 1)
    high_ref[1, place] = jnp.concatenate([ih, -rh], 1)
    low_ref[0, place] = jnp.concatenate([rl, il], 1)
    low_ref[1, place] = jnp.concatenate([il, -rl], 1)


def bin_gram(place, high_ref, low_ref):
    def rows(ref, kind):
        return ref[kind, pl.ds(place, 2)].reshape(128, 2 * TILE)

    ah, al = rows(high_ref, 0), rows(low_ref, 0)
    bh = jnp.concatenate([ah, rows(high_ref, 1)], 0)
    bl = jnp.concatenate([al, rows(low_ref, 1)], 0)
    both = dot3((ah, al), (bh, bl), ((1,), (1,)))
    row = lax.broadcasted_iota(jnp.int32, (128, 128), 0)
    column = lax.broadcasted_iota(jnp.int32, (128, 128), 1)
    return jnp.where(row <= column, both[:, :128], both[:, 128:])


def gram0_kernel(mask_ref, r_ref, sums_ref, spectra_ref, high_ref, low_ref):
    def plant_one(b, carry):
        def store(rh, ih):
            @pl.when(b < BINS)
            def _():
                spectra_ref[0, b] = rh
                spectra_ref[1, b] = ih

        plant(b, r_ref[:, b], store, high_ref, low_ref)
        return carry

    lax.fori_loop(0, WIDE, plant_one, 0, unroll=3)

    def one(b, carry):
        weight = mask_ref[b, 0].astype(F32)
        sums_ref[b] = bin_gram(b, high_ref, low_ref) * weight
        return carry

    lax.fori_loop(0, BINS, one, 0, unroll=4)


def gram_scratch(count):
    return [pltpu.VMEM((2, count + 1, 64, 2 * TILE), BF16)] * 2


def gram0(mask, received):
    return pl.pallas_call(
        gram0_kernel,
        in_specs=[SMEM, VMEM],
        out_specs=[
            VMEM,
            pl.BlockSpec((2, BINS, 64, TILE), lambda i: (0, 0, 0, 0)),
        ],
        grid=(1,),
        out_shape=[
            jax.ShapeDtypeStruct((BINS, 128, 128), F32),
            jax.ShapeDtypeStruct((2, BINS, 64, 2 * TILE), BF16),
        ],
        scratch_shapes=gram_scratch(BINS),
        compiler_params=params(),
        cost_estimate=cost(2e9, 6e6),
        name="gram0",
    )(mask, received)


def gram1_kernel(first, count, split_at, spot_ref, mask_ref, sums_ref, *refs):
    pieces = refs[: len(split_at)]
    _, keep_ref, send_ref, spectra_ref, high_ref, low_ref = refs[len(split_at) :]
    place = 0
    for piece, (start, amount) in zip(pieces, split_at):

        def plant_one(i, carry, piece=piece, start=start, place=place):
            def store(rh, ih):
                @pl.when(place + i < count)
                def _():
                    spectra_ref[0, place + i] = rh
                    spectra_ref[1, place + i] = ih

            plant(place + i, piece[:, start + i], store, high_ref, low_ref)
            return carry

        lax.fori_loop(0, amount, plant_one, 0, unroll=min(amount, 4))
        place += amount
    half = count // 2
    core = spot_ref[1]
    for out_ref, base in ((send_ref, (1 - core) * half), (keep_ref, core * half)):

        def one(i, carry, out_ref=out_ref, base=base):
            b = base + i
            weight = mask_ref[first + b, 1].astype(F32)
            out_ref[i] = sums_ref[b] + bin_gram(b, high_ref, low_ref) * weight
            return carry

        lax.fori_loop(0, half, one, 0, unroll=4)


def gram1(first, count, spot, mask, sums, pieces, split_at, spectra, name):
    half = count // 2
    block = first // count
    return pl.pallas_call(
        functools.partial(gram1_kernel, first, count, split_at),
        grid=(1,),
        in_specs=[
            SMEM,
            SMEM,
            pl.BlockSpec((count, 128, 128), lambda i: (block, 0, 0)),
        ]
        + [VMEM] * len(pieces)
        + [ANY],
        out_specs=[VMEM, VMEM, pl.BlockSpec((2, count, 64, TILE), lambda i: (0, block, 0, 1))],
        out_shape=[
            jax.ShapeDtypeStruct((half, 128, 128), F32),
            jax.ShapeDtypeStruct((half, 128, 128), F32),
            jax.ShapeDtypeStruct(spectra.shape, spectra.dtype),
        ],
        scratch_shapes=gram_scratch(count),
        input_output_aliases={3 + len(pieces): 2},
        compiler_params=params(),
        cost_estimate=cost(2e9 * count / 32, 6e6 * count / 32),
        name=name,
    )(spot, mask, sums, *pieces, spectra)


def core_sum_kernel(share, spot_ref, keep_ref, got_ref, *outs):
    for k, out_ref in enumerate(outs):
        base = lax.rem(spot_ref[0] + k, 4) * share
        out_ref[...] = keep_ref[pl.ds(base, share)] + got_ref[pl.ds(base, share)]


def core_sum(spot, keep, got):
    share = keep.shape[0] // 4
    return pl.pallas_call(
        functools.partial(core_sum_kernel, share),
        in_specs=[SMEM, VMEM, VMEM],
        out_specs=[VMEM] * 4,
        out_shape=[jax.ShapeDtypeStruct((share, 128, 128), F32)] * 4,
        compiler_params=params(),
        cost_estimate=cost(1e6, 2e6),
        name="core_sum",
    )(spot, keep, got)


def factor_kernel(scaling, *refs):
    out_ref = refs[-7]
    ins = refs[:-7]
    gre_ref, gim_ref, fre_ref, fim_ref, sre_ref, sim_ref = refs[-6:]
    count = out_ref.shape[0]
    row = lax.broadcasted_iota(jnp.int32, (128, 128), 0)
    column = lax.broadcasted_iota(jnp.int32, (128, 128), 1)
    for n in range(count):
        packed = ins[0][n]
        for more in ins[1:]:
            packed = packed + more[n]
        packed = packed * scaling
        turned = packed.T
        gre_ref[n] = jnp.where(row <= column, packed, turned)
        gim_ref[n] = jnp.where(row < column, -turned, jnp.where(row > column, packed, 0.0))
    high = lax.Precision.HIGHEST
    dims = (((0,), (0,)), ((), ()))
    dot = functools.partial(
        lax.dot_general, dimension_numbers=dims, preferred_element_type=F32, precision=high
    )
    for offset in range(0, 128, STRIP):
        strips = []
        for n in range(count):
            re = gre_ref[n, offset : offset + STRIP]
            im = gim_ref[n, offset : offset + STRIP]
            if offset:
                fr, fi = fre_ref[n, :offset], fim_ref[n, :offset]
                lr, li = fr[:, offset : offset + STRIP], fi[:, offset : offset + STRIP]
                both = jnp.concatenate([fr, fi], 0)
                re = re - dot(jnp.concatenate([lr, li], 0), both)
                im = im - dot(jnp.concatenate([-li, lr], 0), both)
            strips.append((re, im))
        for i in range(STRIP):
            place = offset + i
            later = []
            for n, (re, im) in enumerate(strips):
                col_re = re[:, place : place + 1]
                col_im = im[:, place : place + 1]
                pivot = re[i : i + 1, place : place + 1]
                inverse = lax.rsqrt(pivot)
                row_re = re[i : i + 1] * inverse
                row_im = im[i : i + 1] * inverse
                fre_ref[n, place : place + 1] = row_re
                fim_ref[n, place : place + 1] = row_im
                if i + 1 < STRIP:
                    cr = col_re * inverse
                    ci = col_im * inverse
                    re, im = (
                        re - (cr * row_re - ci * row_im),
                        im - (cr * row_im + ci * row_re),
                    )
                later.append((re, im))
            strips = later
        for n in range(count):
            fre = fre_ref[n, offset : offset + STRIP]
            fim = fim_ref[n, offset : offset + STRIP]
            r = lax.broadcasted_iota(jnp.int32, (STRIP, 128), 0) + offset
            c = lax.broadcasted_iota(jnp.int32, (STRIP, 128), 1)
            fre_ref[n, offset : offset + STRIP] = jnp.where(c >= r, fre, 0.0)
            fim_ref[n, offset : offset + STRIP] = jnp.where(c > r, fim, 0.0)
    for n in range(count):
        out_ref[n] = fre_ref[n] + fim_ref[n].T


def factor(pieces, scaling):
    count = pieces[0].shape[0]
    return pl.pallas_call(
        functools.partial(factor_kernel, scaling),
        in_specs=[VMEM] * len(pieces),
        out_specs=VMEM,
        out_shape=jax.ShapeDtypeStruct((count, 128, 128), F32),
        scratch_shapes=[pltpu.VMEM((count, 128, 128), F32)] * 4
        + [pltpu.VMEM((count, STRIP, 128), F32)] * 2,
        compiler_params=params(),
        cost_estimate=cost(8e9, 2e6),
        name="factor",
    )(*pieces)


def unpack_kernel(share, spot_ref, *refs):
    pieces, out_ref = refs[:8], refs[-1]
    row = lax.broadcasted_iota(jnp.int32, (128, 128), 0)
    column = lax.broadcasted_iota(jnp.int32, (128, 128), 1)
    y, core = spot_ref[0], spot_ref[1]
    for k in range(8):
        steps, other = k % 4, k // 4
        owner = lax.rem(y + 4 - steps, 4)
        whose = core + other - 2 * core * other
        base = (whose * 4 + owner) * share

        def one(i, carry, piece=pieces[k], base=base):
            packed = piece[i]
            out_ref[base + i, 0] = jnp.where(row <= column, packed, 0.0)
            out_ref[base + i, 1] = jnp.where(row < column, packed.T, 0.0)
            return carry

        lax.fori_loop(0, share, one, 0, unroll=True)


def unpack(first, spot, pieces, below):
    share = pieces[0].shape[0]
    count = share * 8
    block = first // count
    more = [] if below is None else [below]
    return pl.pallas_call(
        functools.partial(unpack_kernel, share),
        grid=(1,),
        in_specs=[SMEM] + [VMEM] * 8 + [ANY] * len(more),
        out_specs=pl.BlockSpec((count, 2, 128, 128), lambda i: (block, 0, 0, 0)),
        out_shape=jax.ShapeDtypeStruct((BINS, 2, 128, 128), F32),
        input_output_aliases={9: 0} if more else {},
        compiler_params=params(),
        cost_estimate=cost(1e6, count * 200e3),
        name="unpack",
    )(spot, *pieces, *more)


def along_y(value, steps):
    return lax.ppermute(value, "range", [(i, (i + 2 * steps) % 8) for i in range(8)])


def other_core(value):
    return lax.ppermute(value, "range", [(i, i ^ 1) for i in range(8)])


def across(value):
    return lax.all_to_all(value, "chan", split_axis=0, concat_axis=0, tiled=True)


def back(spot, keep, send, scaling):
    got = other_core(send)
    own, *rest = core_sum(spot, keep, got)
    parts = [own] + [along_y(piece, k + 1) for k, piece in enumerate(rest)]
    mine = factor(parts, scaling)
    found = [mine] + [along_y(mine, k) for k in (1, 2, 3)]
    return found + [other_core(piece) for piece in found]


def on_device(echoes, chirp, train_mask):
    w = jnp.asarray(doppler_matrices())
    spot_range = lax.axis_index("range").astype(jnp.int32)
    spot = jnp.stack([spot_range // 2, spot_range % 2])
    scaling = 1.0 / (2 * TILE * 8)
    flat0, rim = front0(chirp, echoes, w)
    halo = lax.ppermute(rim, "range", [(i, i - 1) for i in range(1, 8)])
    got0 = across(flat0.reshape(CHANS, WIDE, 8, TILE))
    send_a, send_b = front1(chirp, echoes, halo, w)
    got_a = across(send_a).reshape(CHANS, EARLY + 1, 8, TILE)
    got_b = across(send_b).reshape(CHANS, LATE, 8, TILE)
    sums0, spectra = gram0(train_mask, got0)
    keep_a, out_a, spectra = gram1(
        0, EARLY, spot, train_mask, sums0, [got_a], [(0, EARLY + 1)], spectra, "gram_a"
    )
    pieces_a = back(spot, keep_a, out_a, scaling)
    keep_b, out_b, spectra = gram1(
        EARLY, LATE, spot, train_mask, sums0, [got_a, got_b], [(EARLY, 1), (0, LATE)], spectra, "gram_b"
    )
    pieces_b = back(spot, keep_b, out_b, scaling)
    factors = unpack(0, spot, pieces_a, None)
    factors = unpack(EARLY, spot, pieces_b, factors)
    return spectra, factors


def solution(mesh):
    return jax.shard_map(
        on_device,
        mesh=mesh,
        in_specs=(P(None, "chan", None, "range"), P(), P("chan", "range")),
        out_specs=(P(None, "chan", None, "range"), P("chan", None, None, None)),
        check_vma=False,
    )
```

```python
import functools
import math

import jax
import jax.numpy as jnp
import numpy as np
from jax import lax
from jax.experimental import pallas as pl
from jax.experimental.pallas import tpu as pltpu
from jax.sharding import PartitionSpec as P

PULSES = 512
TILE = 128
BINS = 32
GROUP = 8
WIDE = BINS + 1
CHANS = 16
LOCAL = 4
STRIP = 32
F32 = jnp.float32
BF16 = jnp.bfloat16
VMEM = pl.BlockSpec(memory_space=pltpu.VMEM)
SMEM = pl.BlockSpec(memory_space=pltpu.SMEM)
ANY = pl.BlockSpec(memory_space=pl.ANY)


def params(mib=60):
    return pltpu.CompilerParams(vmem_limit_bytes=mib << 20)


def cost(flops, nbytes):
    return pl.CostEstimate(flops=int(flops), bytes_accessed=int(nbytes), transcendentals=0)


def split(value):
    high = value.astype(BF16)
    return high, (value - high.astype(F32)).astype(BF16)


def dot3(left, right, contract=((1,), (0,))):
    lh, ll = left
    rh, rl = right
    dims = (contract, ((), ()))
    dot = functools.partial(lax.dot_general, dimension_numbers=dims, preferred_element_type=F32)
    return dot(lh, rh) + (dot(lh, rl) + dot(ll, rh))


def doppler_matrices():
    rows = np.arange(128)[:, None]
    pulses = np.arange(128)[None, :]
    found = []
    for j in range(4):
        angle = ((4 * rows + j) * pulses % PULSES) * (2.0 * math.pi / PULSES)
        c, s = np.cos(angle), np.sin(angle)
        found.append(np.block([[c, s], [-s, c]]) / math.sqrt(PULSES))
    full = np.stack(found).astype(np.float32)
    high = full.astype(jnp.bfloat16)
    low = (full - high.astype(np.float32)).astype(jnp.bfloat16)
    return np.stack([high, low])


def fill_toeplitz(chirp_ref, pad_ref, kmat_ref):
    pad_ref[...] = jnp.zeros_like(pad_ref)
    pad_ref[0:2, 0 : TILE + 1] = chirp_ref[...]
    taps = []
    for part in range(2):
        row = jnp.broadcast_to(pad_ref[part : part + 1, :], (TILE, 2 * TILE))
        taps.append(pltpu.roll(row, 0, 1, stride=1, stride_axis=0).T)
    re, im = taps
    full = jnp.concatenate(
        [jnp.concatenate([re, -im], 1), jnp.concatenate([im, re], 1)], 0
    )
    kmat_ref[0], kmat_ref[1] = split(full)


def front_body(step, windows, kmat_ref, w_ref, store):
    tables = (kmat_ref[0], kmat_ref[1])
    quarters = [[], [], [], []]
    for window in windows:
        y = dot3(split(window), tables)
        y0, y1, y2, y3 = (y[128 * q : 128 * q + 128] for q in range(4))
        s02, d02, s13, d13 = y0 + y2, y0 - y2, y1 + y3, y1 - y3
        d02r, d02i, d13r, d13i = d02[:, :128], d02[:, 128:], d13[:, :128], d13[:, 128:]
        z0, z2 = s02 + s13, s02 - s13
        quarters[0].append((z0[:, :128], z0[:, 128:]))
        quarters[1].append((d02r + d13i, d02i - d13r))
        quarters[2].append((z2[:, :128], z2[:, 128:]))
        quarters[3].append((d02r - d13i, d02i + d13r))
    for j in range(4):
        (r0, i0), (r1, i1) = quarters[j]
        data = jnp.concatenate(
            [jnp.concatenate([r0, r1], 1), jnp.concatenate([i0, i1], 1)], 0
        )
        out = dot3((w_ref[0, j], w_ref[1, j]), split(data))
        for part in range(2):
            for c in range(2):
                store(j, part, c, out[128 * part : 128 * part + 128, 128 * c : 128 * c + 128])


def store_into(flat_ref, step):
    def store(j, part, c, block):
        for k in range(CHANS):
            start = k * WIDE * 8 + j * 8 + part * 4 + c + 2 * step
            flat_ref[pl.ds(start, 8, stride=32), :] = block[8 * k : 8 * k + 8]

    return store


def add_edges(flat_ref):
    for k in range(CHANS):
        source = ((k + 1) % CHANS) * WIDE * 8
        flat_ref[pl.ds(k * WIDE * 8 + BINS * 8, 8), :] = flat_ref[pl.ds(source, 8), :]


def front0_kernel(chirp_ref, x_ref, w_ref, out_ref, rim_ref, pad_ref, kmat_ref):
    step = pl.program_id(0)

    @pl.when(step == 0)
    def _():
        fill_toeplitz(chirp_ref, pad_ref, kmat_ref)

    windows = []
    for c in range(2):
        windows.append(jnp.concatenate([x_ref[0, c], x_ref[1, c]], 1))
    rim_ref[...] = x_ref[:, :, :, :TILE]
    front_body(step, windows, kmat_ref, w_ref, store_into(out_ref, step))

    @pl.when(step == 1)
    def _():
        add_edges(out_ref)


def front1_kernel(chirp_ref, x_ref, h_ref, w_ref, out_ref, pad_ref, kmat_ref):
    step = pl.program_id(0)

    @pl.when(step == 0)
    def _():
        fill_toeplitz(chirp_ref, pad_ref, kmat_ref)

    windows = []
    for c in range(2):
        windows.append(jnp.concatenate([x_ref[0, c], h_ref[0, c], x_ref[1, c], h_ref[1, c]], 1))
    front_body(step, windows, kmat_ref, w_ref, store_into(out_ref, step))

    @pl.when(step == 1)
    def _():
        add_edges(out_ref)


def front_scratch():
    return [pltpu.VMEM((8, 2 * TILE), F32), pltpu.VMEM((2, 4 * TILE, 2 * TILE), BF16)]


def front0(chirp, echoes, w):
    return pl.pallas_call(
        front0_kernel,
        grid=(2,),
        in_specs=[
            pl.BlockSpec(chirp.shape, lambda i: (0, 0)),
            pl.BlockSpec((2, 2, PULSES, 2 * TILE), lambda i: (0, i, 0, 0)),
            pl.BlockSpec(w.shape, lambda i: (0, 0, 0, 0)),
        ],
        out_specs=[
            pl.BlockSpec((CHANS * WIDE * 8, TILE), lambda i: (0, 0)),
            pl.BlockSpec((2, 2, PULSES, TILE), lambda i: (0, i, 0, 0)),
        ],
        out_shape=[
            jax.ShapeDtypeStruct((CHANS * WIDE * 8, TILE), F32),
            jax.ShapeDtypeStruct((2, LOCAL, PULSES, TILE), F32),
        ],
        scratch_shapes=front_scratch(),
        compiler_params=params(),
        cost_estimate=cost(4e9, 12e6),
        name="front0",
    )(chirp, echoes, w)


def front1(chirp, echoes, rim, w):
    return pl.pallas_call(
        front1_kernel,
        grid=(2,),
        in_specs=[
            pl.BlockSpec(chirp.shape, lambda i: (0, 0)),
            pl.BlockSpec((2, 2, PULSES, TILE), lambda i: (0, i, 0, 1)),
            pl.BlockSpec((2, 2, PULSES, TILE), lambda i: (0, i, 0, 0)),
            pl.BlockSpec(w.shape, lambda i: (0, 0, 0, 0)),
        ],
        out_specs=pl.BlockSpec((CHANS * WIDE * 8, TILE), lambda i: (0, 0)),
        out_shape=jax.ShapeDtypeStruct((CHANS * WIDE * 8, TILE), F32),
        scratch_shapes=front_scratch(),
        compiler_params=params(),
        cost_estimate=cost(4e9, 8e6),
        name="front1",
    )(chirp, echoes, rim, w)


def unweave(blocks):
    pairs = blocks.reshape(CHANS // 2, 2, 8, TILE)
    even, odd = pairs[:, 0], pairs[:, 1]
    first = lax.broadcasted_iota(jnp.int32, even.shape, 1) < 4
    even_turned = pltpu.roll(even, 4, 1)
    odd_turned = pltpu.roll(odd, 4, 1)
    re = jnp.where(first, even, odd_turned).reshape(CHANS * LOCAL, TILE)
    im = jnp.where(first, even_turned, odd).reshape(CHANS * LOCAL, TILE)
    return re, im


def plant(place, blocks, store_spectra, high_ref, low_ref):
    re, im = unweave(blocks)
    rh, rl = split(re)
    ih, il = split(im)
    store_spectra(rh, ih)
    high_ref[0, place] = jnp.concatenate([rh, ih], 1)
    high_ref[1, place] = jnp.concatenate([ih, -rh], 1)
    low_ref[0, place] = jnp.concatenate([rl, il], 1)
    low_ref[1, place] = jnp.concatenate([il, -rl], 1)


def bin_gram(place, high_ref, low_ref):
    def rows(ref, kind):
        return ref[kind, pl.ds(place, 2)].reshape(128, 2 * TILE)

    ah, al = rows(high_ref, 0), rows(low_ref, 0)
    bh = jnp.concatenate([ah, rows(high_ref, 1)], 0)
    bl = jnp.concatenate([al, rows(low_ref, 1)], 0)
    both = dot3((ah, al), (bh, bl), ((1,), (1,)))
    row = lax.broadcasted_iota(jnp.int32, (128, 128), 0)
    column = lax.broadcasted_iota(jnp.int32, (128, 128), 1)
    return jnp.where(row <= column, both[:, :128], both[:, 128:])


def gram_scratch(count):
    return [pltpu.VMEM((2, count + 1, 64, 2 * TILE), BF16)] * 2


def plant_all(r_ref, edge_ref, spectra_ref, high_ref, low_ref):
    for b in range(GROUP):

        def store(rh, ih, b=b):
            spectra_ref[0, b] = rh
            spectra_ref[1, b] = ih

        plant(b, r_ref[:, b], store, high_ref, low_ref)
    plant(GROUP, edge_ref[:, 0], lambda rh, ih: None, high_ref, low_ref)


def gram0_kernel(mask_ref, r_ref, edge_ref, sums_ref, spectra_ref, high_ref, low_ref):
    first = pl.program_id(0) * GROUP
    plant_all(r_ref, edge_ref, spectra_ref, high_ref, low_ref)
    for b in range(GROUP):
        weight = mask_ref[0, first + b].astype(F32)
        sums_ref[b] = bin_gram(b, high_ref, low_ref) * weight


def gram0(mask, received):
    return pl.pallas_call(
        gram0_kernel,
        grid=(BINS // GROUP,),
        in_specs=[
            SMEM,
            pl.BlockSpec((CHANS, GROUP, 8, TILE), lambda i: (0, i, 0, 0)),
            pl.BlockSpec((CHANS, 1, 8, TILE), lambda i: (0, GROUP * (i + 1), 0, 0)),
        ],
        out_specs=[
            pl.BlockSpec((GROUP, 128, 128), lambda i: (i, 0, 0)),
            pl.BlockSpec((2, GROUP, 64, TILE), lambda i: (0, i, 0, 0)),
        ],
        out_shape=[
            jax.ShapeDtypeStruct((BINS, 128, 128), F32),
            jax.ShapeDtypeStruct((2, BINS, 64, 2 * TILE), BF16),
        ],
        scratch_shapes=gram_scratch(GROUP),
        compiler_params=params(20),
        cost_estimate=cost(2e9, 6e6),
        name="gram0",
    )(mask, received, received)


def gram1_kernel(spot_ref, mask_ref, r_ref, edge_ref, sums_ref, _, send_ref, keep_ref, spectra_ref, high_ref, low_ref):
    steps = BINS // GROUP
    step = pl.program_id(0)
    first = lax.rem(step + (1 - spot_ref[1]) * (steps // 2), steps) * GROUP
    plant_all(r_ref, edge_ref, spectra_ref, high_ref, low_ref)

    def fill(out_ref):
        for b in range(GROUP):
            weight = mask_ref[1, first + b].astype(F32)
            out_ref[b] = sums_ref[b] + bin_gram(b, high_ref, low_ref) * weight

    @pl.when(step < steps // 2)
    def _():
        fill(send_ref)

    @pl.when(step >= steps // 2)
    def _():
        fill(keep_ref)


def gram1(spot, mask, received, sums, spectra):
    steps = BINS // GROUP
    half = steps // 2

    def at(i, spot):
        return lax.rem(i + (1 - spot[1]) * half, steps)

    return pl.pallas_call(
        gram1_kernel,
        grid_spec=pltpu.PrefetchScalarGridSpec(
            num_scalar_prefetch=1,
            grid=(steps,),
            in_specs=[
                SMEM,
                pl.BlockSpec((CHANS, GROUP, 8, TILE), lambda i, spot: (0, at(i, spot), 0, 0)),
                pl.BlockSpec((CHANS, 1, 8, TILE), lambda i, spot: (0, GROUP * (at(i, spot) + 1), 0, 0)),
                pl.BlockSpec((GROUP, 128, 128), lambda i, spot: (at(i, spot), 0, 0)),
                ANY,
            ],
            out_specs=[
                pl.BlockSpec((GROUP, 128, 128), lambda i, spot: (jnp.minimum(i, half - 1), 0, 0)),
                pl.BlockSpec((GROUP, 128, 128), lambda i, spot: (jnp.maximum(i - half, 0), 0, 0)),
                pl.BlockSpec((2, GROUP, 64, TILE), lambda i, spot: (0, at(i, spot), 0, 1)),
            ],
            scratch_shapes=gram_scratch(GROUP),
        ),
        out_shape=[jax.ShapeDtypeStruct((BINS // 2, 128, 128), F32)] * 2
        + [jax.ShapeDtypeStruct(spectra.shape, spectra.dtype)],
        input_output_aliases={5: 2},
        compiler_params=params(20),
        cost_estimate=cost(2e9, 6e6),
        name="gram1",
    )(spot, mask, received, received, sums, spectra)


def core_sum_kernel(share, spot_ref, keep_ref, got_ref, *outs):
    for k, out_ref in enumerate(outs):
        base = lax.rem(spot_ref[0] + k, 4) * share
        out_ref[...] = keep_ref[pl.ds(base, share)] + got_ref[pl.ds(base, share)]


def core_sum(spot, keep, got):
    share = keep.shape[0] // 4
    return pl.pallas_call(
        functools.partial(core_sum_kernel, share),
        in_specs=[SMEM, VMEM, VMEM],
        out_specs=[VMEM] * 4,
        out_shape=[jax.ShapeDtypeStruct((share, 128, 128), F32)] * 4,
        compiler_params=params(16),
        cost_estimate=cost(1e6, 1e5),
        name="core_sum",
    )(spot, keep, got)


def spread(value):
    return jnp.broadcast_to(value, (8, 128))


def minus(value, left, right):
    re, im = value
    lr, li = left
    rr, ri = right
    return re - (lr * rr - li * ri), im - (lr * ri + li * rr)


def conj(value):
    return value[0], -value[1]


def four_columns(groups, i, place, store_row, last):
    columns = [
        [(spread(re[:, place + v : place + v + 1]), spread(im[:, place + v : place + v + 1])) for re, im in groups]
        for v in range(4)
    ]
    g, r = divmod(i, 8)
    corner = {}
    for u in range(4):
        for v in range(u, 4):
            re, im = columns[v][g]
            corner[u, v] = spread(re[r + u : r + u + 1]), spread(im[r + u : r + u + 1])
    re, im = groups[g]
    rows = [(spread(re[r + u : r + u + 1]), spread(im[r + u : r + u + 1])) for u in range(4)]
    inverses, upper = [], {}
    for t in range(4):
        inverse = lax.rsqrt(corner[t, t][0])
        inverses.append(inverse)
        for v in range(t + 1, 4):
            upper[t, v] = corner[t, v][0] * inverse, corner[t, v][1] * inverse
        for u in range(t + 1, 4):
            for v in range(u, 4):
                corner[u, v] = minus(corner[u, v], conj(upper[t, u]), upper[t, v])
    found = []
    for t in range(4):
        value = rows[t]
        for u in range(t):
            value = minus(value, conj(upper[u, t]), found[u])
        found.append((value[0] * inverses[t], value[1] * inverses[t]))
        store_row(place + t, found[t][0][0:1], found[t][1][0:1])
    if last:
        return groups
    later = []
    for g, value in enumerate(groups):
        if 8 * g + 8 > i + 4:
            scaled = []
            for t in range(4):
                column = columns[t][g]
                for u in range(t):
                    column = minus(column, scaled[u], upper[u, t])
                scaled.append((column[0] * inverses[t], column[1] * inverses[t]))
            for t in range(4):
                value = minus(value, scaled[t], found[t])
        later.append(value)
    return later


def factor_kernel(scaling, *refs):
    out_ref, gre_ref, gim_ref, fre_ref, fim_ref = refs[-5:]
    ins = refs[:-5]
    count = out_ref.shape[0]
    row = lax.broadcasted_iota(jnp.int32, (128, 128), 0)
    column = lax.broadcasted_iota(jnp.int32, (128, 128), 1)
    for n in range(count):
        packed = ins[0][n]
        for more in ins[1:]:
            packed = packed + more[n]
        packed = packed * scaling
        turned = packed.T
        gre_ref[n] = jnp.where(row <= column, packed, turned)
        gim_ref[n] = jnp.where(row < column, -turned, jnp.where(row > column, packed, 0.0))
    dims = (((0,), (0,)), ((), ()))
    dot = functools.partial(
        lax.dot_general,
        dimension_numbers=dims,
        preferred_element_type=F32,
        precision=lax.Precision.HIGHEST,
    )
    for offset in range(0, 128, STRIP):
        strips = []
        for n in range(count):
            re = gre_ref[n, offset : offset + STRIP]
            im = gim_ref[n, offset : offset + STRIP]
            if offset:
                fr, fi = fre_ref[n, :offset], fim_ref[n, :offset]
                lr, li = fr[:, offset : offset + STRIP], fi[:, offset : offset + STRIP]
                left = jnp.concatenate(
                    [jnp.concatenate([lr, -li], 1), jnp.concatenate([li, lr], 1)], 0
                )
                update = dot(left, jnp.concatenate([fr, fi], 0))
                re = re - update[:STRIP]
                im = im - update[STRIP:]
            strips.append([(re[8 * g : 8 * g + 8], im[8 * g : 8 * g + 8]) for g in range(STRIP // 8)])
        for i in range(0, STRIP, 4):
            for n in range(count):

                def store_row(place, re, im, n=n):
                    fre_ref[n, place : place + 1] = re
                    fim_ref[n, place : place + 1] = im

                strips[n] = four_columns(strips[n], i, offset + i, store_row, i + 4 == STRIP)
        r = lax.broadcasted_iota(jnp.int32, (STRIP, 128), 0) + offset
        c = lax.broadcasted_iota(jnp.int32, (STRIP, 128), 1)
        for n in range(count):
            here = slice(offset, offset + STRIP)
            fre_ref[n, here] = jnp.where(c >= r, fre_ref[n, here], 0.0)
            fim_ref[n, here] = jnp.where(c > r, fim_ref[n, here], 0.0)
    for n in range(count):
        out_ref[n] = fre_ref[n] + fim_ref[n].T


def factor(pieces, scaling):
    count = pieces[0].shape[0]
    return pl.pallas_call(
        functools.partial(factor_kernel, scaling),
        in_specs=[VMEM] * len(pieces),
        out_specs=VMEM,
        out_shape=jax.ShapeDtypeStruct((count, 128, 128), F32),
        scratch_shapes=[pltpu.VMEM((count, 128, 128), F32)] * 4,
        compiler_params=params(16),
        cost_estimate=cost(1e6, 1e5),
        name="factor",
    )(*pieces)


def unpack_kernel(share, spot_ref, *refs):
    pieces, out_ref = refs[:8], refs[-1]
    row = lax.broadcasted_iota(jnp.int32, (128, 128), 0)
    column = lax.broadcasted_iota(jnp.int32, (128, 128), 1)
    y, core = spot_ref[0], spot_ref[1]
    for k in range(8):
        steps, other = k % 4, k // 4
        owner = lax.rem(y + 4 - steps, 4)
        whose = core + other - 2 * core * other
        base = (whose * 4 + owner) * share

        def one(i, carry, piece=pieces[k], base=base):
            packed = piece[i]
            out_ref[base + i, 0] = jnp.where(row <= column, packed, 0.0)
            out_ref[base + i, 1] = jnp.where(row < column, packed.T, 0.0)
            return carry

        lax.fori_loop(0, share, one, 0, unroll=True)


def unpack(spot, pieces):
    share = pieces[0].shape[0]
    return pl.pallas_call(
        functools.partial(unpack_kernel, share),
        in_specs=[SMEM] + [VMEM] * 8,
        out_specs=VMEM,
        out_shape=jax.ShapeDtypeStruct((BINS, 2, 128, 128), F32),
        compiler_params=params(16),
        cost_estimate=cost(1e6, 1e5),
        name="unpack",
    )(spot, *pieces)


def along_y(value, steps):
    return lax.ppermute(value, "range", [(i, (i + 2 * steps) % 8) for i in range(8)])


def other_core(value):
    return lax.ppermute(value, "range", [(i, i ^ 1) for i in range(8)])


def across(value):
    return lax.all_to_all(value, "chan", split_axis=0, concat_axis=0, tiled=True)


def gather_sums(spot, keep, send):
    got = other_core(send)
    own, *rest = core_sum(spot, keep, got)
    return [own] + [along_y(piece, k + 1) for k, piece in enumerate(rest)]


def share_factors(mine):
    found = [mine] + [along_y(mine, k) for k in (1, 2, 3)]
    return found + [other_core(piece) for piece in found]


def on_device(echoes, chirp, train_mask):
    w = jnp.asarray(doppler_matrices())
    mask = train_mask.T
    here = lax.axis_index("range").astype(jnp.int32)
    spot = jnp.stack([here >> 1, here & 1])
    scaling = 1.0 / (2 * TILE * lax.axis_size("range"))
    flat0, rim = front0(chirp, echoes, w)
    halo = lax.ppermute(rim, "range", [(i, i - 1) for i in range(1, 8)])
    got0 = across(flat0.reshape(CHANS, WIDE, 8, TILE))
    got1 = across(front1(chirp, echoes, halo, w).reshape(CHANS, WIDE, 8, TILE))
    sums0, spectra = gram0(mask, got0)
    send, keep, spectra = gram1(spot, mask, got1, sums0, spectra)
    mine = factor(gather_sums(spot, keep, send), scaling)
    factors = unpack(spot, share_factors(mine))
    return spectra, factors


def solution(mesh):
    return jax.shard_map(
        on_device,
        mesh=mesh,
        in_specs=(P(None, "chan", None, "range"), P(), P("chan", "range")),
        out_specs=(P(None, "chan", None, "range"), P("chan", None, None, None)),
        check_vma=False,
    )
```

```python
import functools
import math

import jax
import jax.numpy as jnp
import numpy as np
from jax import lax
from jax.experimental import pallas as pl
from jax.experimental.pallas import tpu as pltpu
from jax.sharding import PartitionSpec as P

PULSES = 512
TILE = 128
BINS = 32
GROUP = 8
WIDE = BINS + 1
CHANS = 16
LOCAL = 4
STRIP = 32
F32 = jnp.float32
BF16 = jnp.bfloat16
VMEM = pl.BlockSpec(memory_space=pltpu.VMEM)
SMEM = pl.BlockSpec(memory_space=pltpu.SMEM)
ANY = pl.BlockSpec(memory_space=pl.ANY)


def params(mib=60):
    return pltpu.CompilerParams(vmem_limit_bytes=mib << 20)


def cost(flops, nbytes):
    return pl.CostEstimate(flops=int(flops), bytes_accessed=int(nbytes), transcendentals=0)


def split(value):
    high = value.astype(BF16)
    return high, (value - high.astype(F32)).astype(BF16)


def dot3(left, right, contract=((1,), (0,))):
    lh, ll = left
    rh, rl = right
    dims = (contract, ((), ()))
    dot = functools.partial(lax.dot_general, dimension_numbers=dims, preferred_element_type=F32)
    return dot(lh, rh) + (dot(lh, rl) + dot(ll, rh))


def doppler_matrices():
    rows = np.arange(128)[:, None]
    pulses = np.arange(128)[None, :]
    found = []
    for j in range(4):
        angle = ((4 * rows + j) * pulses % PULSES) * (2.0 * math.pi / PULSES)
        c, s = np.cos(angle), np.sin(angle)
        found.append(np.block([[c, s], [-s, c]]) / math.sqrt(PULSES))
    full = np.stack(found).astype(np.float32)
    high = full.astype(jnp.bfloat16)
    low = (full - high.astype(np.float32)).astype(jnp.bfloat16)
    return np.stack([high, low])


def fill_toeplitz(chirp_ref, pad_ref, kmat_ref):
    pad_ref[...] = jnp.zeros_like(pad_ref)
    pad_ref[0:2, 0 : TILE + 1] = chirp_ref[...]
    taps = []
    for part in range(2):
        row = jnp.broadcast_to(pad_ref[part : part + 1, :], (TILE, 2 * TILE))
        taps.append(pltpu.roll(row, 0, 1, stride=1, stride_axis=0).T)
    re, im = taps
    full = jnp.concatenate(
        [jnp.concatenate([re, -im], 1), jnp.concatenate([im, re], 1)], 0
    )
    kmat_ref[0], kmat_ref[1] = split(full)


def front_body(step, windows, kmat_ref, w_ref, store):
    tables = (kmat_ref[0], kmat_ref[1])
    quarters = [[], [], [], []]
    for window in windows:
        y = dot3(split(window), tables)
        y0, y1, y2, y3 = (y[128 * q : 128 * q + 128] for q in range(4))
        s02, d02, s13, d13 = y0 + y2, y0 - y2, y1 + y3, y1 - y3
        d02r, d02i, d13r, d13i = d02[:, :128], d02[:, 128:], d13[:, :128], d13[:, 128:]
        z0, z2 = s02 + s13, s02 - s13
        quarters[0].append((z0[:, :128], z0[:, 128:]))
        quarters[1].append((d02r + d13i, d02i - d13r))
        quarters[2].append((z2[:, :128], z2[:, 128:]))
        quarters[3].append((d02r - d13i, d02i + d13r))
    for j in range(4):
        (r0, i0), (r1, i1) = quarters[j]
        data = jnp.concatenate(
            [jnp.concatenate([r0, r1], 1), jnp.concatenate([i0, i1], 1)], 0
        )
        out = dot3((w_ref[0, j], w_ref[1, j]), split(data))
        for part in range(2):
            for c in range(2):
                store(j, part, c, out[128 * part : 128 * part + 128, 128 * c : 128 * c + 128])


def store_into(flat_ref, step):
    def store(j, part, c, block):
        for k in range(CHANS):
            start = k * WIDE * 8 + j * 8 + part * 4 + c + 2 * step
            flat_ref[pl.ds(start, 8, stride=32), :] = block[8 * k : 8 * k + 8]

    return store


def add_edges(flat_ref):
    for k in range(CHANS):
        source = ((k + 1) % CHANS) * WIDE * 8
        flat_ref[pl.ds(k * WIDE * 8 + BINS * 8, 8), :] = flat_ref[pl.ds(source, 8), :]


def front0_kernel(chirp_ref, x_ref, w_ref, out_ref, rim_ref, pad_ref, kmat_ref):
    step = pl.program_id(0)

    @pl.when(step == 0)
    def _():
        fill_toeplitz(chirp_ref, pad_ref, kmat_ref)

    windows = []
    for c in range(2):
        windows.append(jnp.concatenate([x_ref[0, c], x_ref[1, c]], 1))
    rim_ref[...] = x_ref[:, :, :, :TILE]
    front_body(step, windows, kmat_ref, w_ref, store_into(out_ref, step))

    @pl.when(step == 1)
    def _():
        add_edges(out_ref)


def front1_kernel(chirp_ref, x_ref, h_ref, w_ref, out_ref, pad_ref, kmat_ref):
    step = pl.program_id(0)

    @pl.when(step == 0)
    def _():
        fill_toeplitz(chirp_ref, pad_ref, kmat_ref)

    windows = []
    for c in range(2):
        windows.append(jnp.concatenate([x_ref[0, c], h_ref[0, c], x_ref[1, c], h_ref[1, c]], 1))
    front_body(step, windows, kmat_ref, w_ref, store_into(out_ref, step))

    @pl.when(step == 1)
    def _():
        add_edges(out_ref)


def front_scratch():
    return [pltpu.VMEM((8, 2 * TILE), F32), pltpu.VMEM((2, 4 * TILE, 2 * TILE), BF16)]


def front0(chirp, echoes, w):
    return pl.pallas_call(
        front0_kernel,
        grid=(2,),
        in_specs=[
            pl.BlockSpec(chirp.shape, lambda i: (0, 0)),
            pl.BlockSpec((2, 2, PULSES, 2 * TILE), lambda i: (0, i, 0, 0)),
            pl.BlockSpec(w.shape, lambda i: (0, 0, 0, 0)),
        ],
        out_specs=[
            pl.BlockSpec((CHANS * WIDE * 8, TILE), lambda i: (0, 0)),
            pl.BlockSpec((2, 2, PULSES, TILE), lambda i: (0, i, 0, 0)),
        ],
        out_shape=[
            jax.ShapeDtypeStruct((CHANS * WIDE * 8, TILE), F32),
            jax.ShapeDtypeStruct((2, LOCAL, PULSES, TILE), F32),
        ],
        scratch_shapes=front_scratch(),
        compiler_params=params(),
        cost_estimate=cost(4e9, 12e6),
        name="front0",
    )(chirp, echoes, w)


def front1(chirp, echoes, rim, w):
    return pl.pallas_call(
        front1_kernel,
        grid=(2,),
        in_specs=[
            pl.BlockSpec(chirp.shape, lambda i: (0, 0)),
            pl.BlockSpec((2, 2, PULSES, TILE), lambda i: (0, i, 0, 1)),
            pl.BlockSpec((2, 2, PULSES, TILE), lambda i: (0, i, 0, 0)),
            pl.BlockSpec(w.shape, lambda i: (0, 0, 0, 0)),
        ],
        out_specs=pl.BlockSpec((CHANS * WIDE * 8, TILE), lambda i: (0, 0)),
        out_shape=jax.ShapeDtypeStruct((CHANS * WIDE * 8, TILE), F32),
        scratch_shapes=front_scratch(),
        compiler_params=params(),
        cost_estimate=cost(4e9, 8e6),
        name="front1",
    )(chirp, echoes, rim, w)


def unweave(blocks):
    pairs = blocks.reshape(CHANS // 2, 2, 8, TILE)
    even, odd = pairs[:, 0], pairs[:, 1]
    first = lax.broadcasted_iota(jnp.int32, even.shape, 1) < 4
    even_turned = pltpu.roll(even, 4, 1)
    odd_turned = pltpu.roll(odd, 4, 1)
    re = jnp.where(first, even, odd_turned).reshape(CHANS * LOCAL, TILE)
    im = jnp.where(first, even_turned, odd).reshape(CHANS * LOCAL, TILE)
    return re, im


def plant(place, blocks, store_spectra, high_ref, low_ref):
    re, im = unweave(blocks)
    rh, rl = split(re)
    ih, il = split(im)
    store_spectra(rh, ih)
    high_ref[0, place] = jnp.concatenate([rh, ih], 1)
    high_ref[1, place] = jnp.concatenate([ih, -rh], 1)
    low_ref[0, place] = jnp.concatenate([rl, il], 1)
    low_ref[1, place] = jnp.concatenate([il, -rl], 1)


def bin_gram(place, high_ref, low_ref):
    def rows(ref, kind):
        return ref[kind, pl.ds(place, 2)].reshape(128, 2 * TILE)

    ah, al = rows(high_ref, 0), rows(low_ref, 0)
    bh = jnp.concatenate([ah, rows(high_ref, 1)], 0)
    bl = jnp.concatenate([al, rows(low_ref, 1)], 0)
    both = dot3((ah, al), (bh, bl), ((1,), (1,)))
    row = lax.broadcasted_iota(jnp.int32, (128, 128), 0)
    column = lax.broadcasted_iota(jnp.int32, (128, 128), 1)
    return jnp.where(row <= column, both[:, :128], both[:, 128:])


def gram_scratch(count):
    return [pltpu.VMEM((2, count + 1, 64, 2 * TILE), BF16)] * 2


def plant_all(r_ref, edge_ref, spectra_ref, high_ref, low_ref):
    for b in range(GROUP):

        def store(rh, ih, b=b):
            spectra_ref[0, b] = rh
            spectra_ref[1, b] = ih

        plant(b, r_ref[:, b], store, high_ref, low_ref)
    plant(GROUP, edge_ref[:, 0], lambda rh, ih: None, high_ref, low_ref)


def gram0_kernel(mask_ref, r_ref, edge_ref, sums_ref, spectra_ref, high_ref, low_ref):
    first = pl.program_id(0) * GROUP
    plant_all(r_ref, edge_ref, spectra_ref, high_ref, low_ref)
    for b in range(GROUP):
        weight = mask_ref[0, first + b].astype(F32)
        sums_ref[b] = bin_gram(b, high_ref, low_ref) * weight


def gram0(mask, received):
    return pl.pallas_call(
        gram0_kernel,
        grid=(BINS // GROUP,),
        in_specs=[
            SMEM,
            pl.BlockSpec((CHANS, GROUP, 8, TILE), lambda i: (0, i, 0, 0)),
            pl.BlockSpec((CHANS, 1, 8, TILE), lambda i: (0, GROUP * (i + 1), 0, 0)),
        ],
        out_specs=[
            pl.BlockSpec((GROUP, 128, 128), lambda i: (i, 0, 0)),
            pl.BlockSpec((2, GROUP, 64, TILE), lambda i: (0, i, 0, 0)),
        ],
        out_shape=[
            jax.ShapeDtypeStruct((BINS, 128, 128), F32),
            jax.ShapeDtypeStruct((2, BINS, 64, 2 * TILE), BF16),
        ],
        scratch_shapes=gram_scratch(GROUP),
        compiler_params=params(20),
        cost_estimate=cost(2e9, 6e6),
        name="gram0",
    )(mask, received, received)


def gram1_kernel(other, spot_ref, mask_ref, r_ref, edge_ref, sums_ref, _, out_ref, spectra_ref, high_ref, low_ref):
    core = spot_ref[1]
    half = BINS // GROUP // 2
    first = ((1 - core if other else core) * half + pl.program_id(0)) * GROUP
    plant_all(r_ref, edge_ref, spectra_ref, high_ref, low_ref)
    for b in range(GROUP):
        weight = mask_ref[1, first + b].astype(F32)
        out_ref[b] = sums_ref[b] + bin_gram(b, high_ref, low_ref) * weight


def gram1(other, spot, mask, received, sums, spectra, name):
    half = BINS // GROUP // 2

    def at(i, spot):
        return (1 - spot[1] if other else spot[1]) * half + i

    return pl.pallas_call(
        functools.partial(gram1_kernel, other),
        grid_spec=pltpu.PrefetchScalarGridSpec(
            num_scalar_prefetch=1,
            grid=(half,),
            in_specs=[
                SMEM,
                pl.BlockSpec((CHANS, GROUP, 8, TILE), lambda i, spot: (0, at(i, spot), 0, 0)),
                pl.BlockSpec((CHANS, 1, 8, TILE), lambda i, spot: (0, GROUP * (at(i, spot) + 1), 0, 0)),
                pl.BlockSpec((GROUP, 128, 128), lambda i, spot: (at(i, spot), 0, 0)),
                ANY,
            ],
            out_specs=[
                pl.BlockSpec((GROUP, 128, 128), lambda i, spot: (i, 0, 0)),
                pl.BlockSpec((2, GROUP, 64, TILE), lambda i, spot: (0, at(i, spot), 0, 1)),
            ],
            scratch_shapes=gram_scratch(GROUP),
        ),
        out_shape=[
            jax.ShapeDtypeStruct((BINS // 2, 128, 128), F32),
            jax.ShapeDtypeStruct(spectra.shape, spectra.dtype),
        ],
        input_output_aliases={5: 1},
        compiler_params=params(20),
        cost_estimate=cost(2e9, 6e6),
        name=name,
    )(spot, mask, received, received, sums, spectra)


def core_sum_kernel(share, spot_ref, keep_ref, got_ref, *outs):
    for k, out_ref in enumerate(outs):
        base = lax.rem(spot_ref[0] + k, 4) * share
        out_ref[...] = keep_ref[pl.ds(base, share)] + got_ref[pl.ds(base, share)]


def core_sum(spot, keep, got):
    share = keep.shape[0] // 4
    return pl.pallas_call(
        functools.partial(core_sum_kernel, share),
        in_specs=[SMEM, VMEM, VMEM],
        out_specs=[VMEM] * 4,
        out_shape=[jax.ShapeDtypeStruct((share, 128, 128), F32)] * 4,
        compiler_params=params(16),
        cost_estimate=cost(1e6, 1e5),
        name="core_sum",
    )(spot, keep, got)


def spread(value):
    return jnp.broadcast_to(value, (8, 128))


def minus(value, left, right):
    re, im = value
    lr, li = left
    rr, ri = right
    return re - (lr * rr - li * ri), im - (lr * ri + li * rr)


def conj(value):
    return value[0], -value[1]


def four_columns(groups, i, place, store_row, last):
    columns = [
        [(spread(re[:, place + v : place + v + 1]), spread(im[:, place + v : place + v + 1])) for re, im in groups]
        for v in range(4)
    ]
    g, r = divmod(i, 8)
    corner = {}
    for u in range(4):
        for v in range(u, 4):
            re, im = columns[v][g]
            corner[u, v] = spread(re[r + u : r + u + 1]), spread(im[r + u : r + u + 1])
    re, im = groups[g]
    rows = [(spread(re[r + u : r + u + 1]), spread(im[r + u : r + u + 1])) for u in range(4)]
    inverses, upper = [], {}
    for t in range(4):
        inverse = lax.rsqrt(corner[t, t][0])
        inverses.append(inverse)
        for v in range(t + 1, 4):
            upper[t, v] = corner[t, v][0] * inverse, corner[t, v][1] * inverse
        for u in range(t + 1, 4):
            for v in range(u, 4):
                corner[u, v] = minus(corner[u, v], conj(upper[t, u]), upper[t, v])
    found = []
    for t in range(4):
        value = rows[t]
        for u in range(t):
            value = minus(value, conj(upper[u, t]), found[u])
        found.append((value[0] * inverses[t], value[1] * inverses[t]))
        store_row(place + t, found[t][0][0:1], found[t][1][0:1])
    if last:
        return groups
    later = []
    for g, value in enumerate(groups):
        if 8 * g + 8 > i + 4:
            scaled = []
            for t in range(4):
                column = columns[t][g]
                for u in range(t):
                    column = minus(column, scaled[u], upper[u, t])
                scaled.append((column[0] * inverses[t], column[1] * inverses[t]))
            for t in range(4):
                value = minus(value, scaled[t], found[t])
        later.append(value)
    return later


def factor_kernel(scaling, *refs):
    out_ref, gre_ref, gim_ref, fre_ref, fim_ref = refs[-5:]
    ins = refs[:-5]
    count = out_ref.shape[0]
    row = lax.broadcasted_iota(jnp.int32, (128, 128), 0)
    column = lax.broadcasted_iota(jnp.int32, (128, 128), 1)
    for n in range(count):
        packed = ins[0][n]
        for more in ins[1:]:
            packed = packed + more[n]
        packed = packed * scaling
        turned = packed.T
        gre_ref[n] = jnp.where(row <= column, packed, turned)
        gim_ref[n] = jnp.where(row < column, -turned, jnp.where(row > column, packed, 0.0))
    dims = (((0,), (0,)), ((), ()))
    dot = functools.partial(
        lax.dot_general,
        dimension_numbers=dims,
        preferred_element_type=F32,
        precision=lax.Precision.HIGHEST,
    )
    for offset in range(0, 128, STRIP):
        strips = []
        for n in range(count):
            re = gre_ref[n, offset : offset + STRIP]
            im = gim_ref[n, offset : offset + STRIP]
            if offset:
                fr, fi = fre_ref[n, :offset], fim_ref[n, :offset]
                lr, li = fr[:, offset : offset + STRIP], fi[:, offset : offset + STRIP]
                left = jnp.concatenate(
                    [jnp.concatenate([lr, -li], 1), jnp.concatenate([li, lr], 1)], 0
                )
                update = dot(left, jnp.concatenate([fr, fi], 0))
                re = re - update[:STRIP]
                im = im - update[STRIP:]
            strips.append([(re[8 * g : 8 * g + 8], im[8 * g : 8 * g + 8]) for g in range(STRIP // 8)])
        for i in range(0, STRIP, 4):
            for n in range(count):

                def store_row(place, re, im, n=n):
                    fre_ref[n, place : place + 1] = re
                    fim_ref[n, place : place + 1] = im

                strips[n] = four_columns(strips[n], i, offset + i, store_row, i + 4 == STRIP)
        r = lax.broadcasted_iota(jnp.int32, (STRIP, 128), 0) + offset
        c = lax.broadcasted_iota(jnp.int32, (STRIP, 128), 1)
        for n in range(count):
            here = slice(offset, offset + STRIP)
            fre_ref[n, here] = jnp.where(c >= r, fre_ref[n, here], 0.0)
            fim_ref[n, here] = jnp.where(c > r, fim_ref[n, here], 0.0)
    for n in range(count):
        out_ref[n] = fre_ref[n] + fim_ref[n].T


def factor(pieces, scaling):
    count = pieces[0].shape[0]
    return pl.pallas_call(
        functools.partial(factor_kernel, scaling),
        in_specs=[VMEM] * len(pieces),
        out_specs=VMEM,
        out_shape=jax.ShapeDtypeStruct((count, 128, 128), F32),
        scratch_shapes=[pltpu.VMEM((count, 128, 128), F32)] * 4,
        compiler_params=params(16),
        cost_estimate=cost(1e6, 1e5),
        name="factor",
    )(*pieces)


def unpack_kernel(share, spot_ref, *refs):
    pieces, out_ref, held_ref, sems = refs[:8], refs[8], refs[9], refs[10]
    row = lax.broadcasted_iota(jnp.int32, (128, 128), 0)
    column = lax.broadcasted_iota(jnp.int32, (128, 128), 1)
    y, core = spot_ref[0], spot_ref[1]
    copies = []
    for k in range(8):
        steps, other = k % 4, k // 4
        owner = lax.rem(y + 4 - steps, 4)
        whose = core + other - 2 * core * other
        base = (whose * 4 + owner) * share
        for i in range(share):
            packed = pieces[k][i]
            held_ref[k * share + i, 0] = jnp.where(row <= column, packed, 0.0)
            held_ref[k * share + i, 1] = jnp.where(row < column, packed.T, 0.0)
        copy = pltpu.make_async_copy(
            held_ref.at[pl.ds(k * share, share)], out_ref.at[pl.ds(base, share)], sems.at[k]
        )
        copy.start()
        copies.append(copy)
    for copy in copies:
        copy.wait()


def unpack(spot, pieces):
    share = pieces[0].shape[0]
    return pl.pallas_call(
        functools.partial(unpack_kernel, share),
        in_specs=[SMEM] + [VMEM] * 8,
        out_specs=ANY,
        out_shape=jax.ShapeDtypeStruct((BINS, 2, 128, 128), F32),
        scratch_shapes=[
            pltpu.VMEM((8 * share, 2, 128, 128), F32),
            pltpu.SemaphoreType.DMA((8,)),
        ],
        compiler_params=params(16),
        cost_estimate=cost(1e6, 1e5),
        name="unpack",
    )(spot, *pieces)


def along_y(value, steps):
    return lax.ppermute(value, "range", [(i, (i + 2 * steps) % 8) for i in range(8)])


def other_core(value):
    return lax.ppermute(value, "range", [(i, i ^ 1) for i in range(8)])


def across(value):
    return lax.all_to_all(value, "chan", split_axis=0, concat_axis=0, tiled=True)


def gather_sums(spot, keep, send):
    got = other_core(send)
    own, *rest = core_sum(spot, keep, got)
    return [own] + [along_y(piece, k + 1) for k, piece in enumerate(rest)]


def share_factors(mine):
    found = [mine] + [along_y(mine, k) for k in (1, 2, 3)]
    return found + [other_core(piece) for piece in found]


def on_device(echoes, chirp, train_mask):
    w = jnp.asarray(doppler_matrices())
    mask = train_mask.T
    here = lax.axis_index("range").astype(jnp.int32)
    spot = jnp.stack([here >> 1, here & 1])
    scaling = 1.0 / (2 * TILE * lax.axis_size("range"))
    flat0, rim = front0(chirp, echoes, w)
    halo = lax.ppermute(rim, "range", [(i, i - 1) for i in range(1, 8)])
    got0 = across(flat0.reshape(CHANS, WIDE, 8, TILE))
    got1 = across(front1(chirp, echoes, halo, w).reshape(CHANS, WIDE, 8, TILE))
    sums0, spectra = gram0(mask, got0)
    send, spectra = gram1(True, spot, mask, got1, sums0, spectra, "gram1_send")
    keep, spectra = gram1(False, spot, mask, got1, sums0, spectra, "gram1_keep")
    mine = factor(gather_sums(spot, keep, send), scaling)
    factors = unpack(spot, share_factors(mine))
    return spectra, factors


def solution(mesh):
    return jax.shard_map(
        on_device,
        mesh=mesh,
        in_specs=(P(None, "chan", None, "range"), P(), P("chan", "range")),
        out_specs=(P(None, "chan", None, "range"), P("chan", None, None, None)),
        check_vma=False,
    )
```

```python
import functools
import math

import jax
import jax.numpy as jnp
import numpy as np
from jax import lax
from jax.experimental import pallas as pl
from jax.experimental.pallas import tpu as pltpu
from jax.sharding import PartitionSpec as P

PULSES = 512
TILE = 128
BINS = 32
GROUP = 8
WIDE = BINS + 1
CHANS = 16
LOCAL = 4
STRIP = 32
F32 = jnp.float32
BF16 = jnp.bfloat16
VMEM = pl.BlockSpec(memory_space=pltpu.VMEM)
SMEM = pl.BlockSpec(memory_space=pltpu.SMEM)
ANY = pl.BlockSpec(memory_space=pl.ANY)


def params(mib=60):
    return pltpu.CompilerParams(vmem_limit_bytes=mib << 20)


def cost(flops, nbytes):
    return pl.CostEstimate(flops=int(flops), bytes_accessed=int(nbytes), transcendentals=0)


def split(value):
    high = value.astype(BF16)
    return high, (value - high.astype(F32)).astype(BF16)


def dot3(left, right, contract=((1,), (0,))):
    lh, ll = left
    rh, rl = right
    dims = (contract, ((), ()))
    dot = functools.partial(lax.dot_general, dimension_numbers=dims, preferred_element_type=F32)
    return dot(lh, rh) + (dot(lh, rl) + dot(ll, rh))


def doppler_matrices():
    rows = np.arange(128)[:, None]
    pulses = np.arange(128)[None, :]
    found = []
    for j in range(4):
        angle = ((4 * rows + j) * pulses % PULSES) * (2.0 * math.pi / PULSES)
        c, s = np.cos(angle), np.sin(angle)
        found.append(np.block([[c, s], [-s, c]]) / math.sqrt(PULSES))
    full = np.stack(found).astype(np.float32)
    high = full.astype(jnp.bfloat16)
    low = (full - high.astype(np.float32)).astype(jnp.bfloat16)
    return np.stack([high, low])


def fill_toeplitz(chirp_ref, pad_ref, kmat_ref):
    pad_ref[...] = jnp.zeros_like(pad_ref)
    pad_ref[0:2, 0 : TILE + 1] = chirp_ref[...]
    taps = []
    for part in range(2):
        row = jnp.broadcast_to(pad_ref[part : part + 1, :], (TILE, 2 * TILE))
        taps.append(pltpu.roll(row, 0, 1, stride=1, stride_axis=0).T)
    re, im = taps
    full = jnp.concatenate(
        [jnp.concatenate([re, -im], 1), jnp.concatenate([im, re], 1)], 0
    )
    kmat_ref[0], kmat_ref[1] = split(full)


def front_body(step, windows, kmat_ref, w_ref, store):
    tables = (kmat_ref[0], kmat_ref[1])
    quarters = [[], [], [], []]
    for window in windows:
        y = dot3(split(window), tables)
        y0, y1, y2, y3 = (y[128 * q : 128 * q + 128] for q in range(4))
        s02, d02, s13, d13 = y0 + y2, y0 - y2, y1 + y3, y1 - y3
        d02r, d02i, d13r, d13i = d02[:, :128], d02[:, 128:], d13[:, :128], d13[:, 128:]
        z0, z2 = s02 + s13, s02 - s13
        quarters[0].append((z0[:, :128], z0[:, 128:]))
        quarters[1].append((d02r + d13i, d02i - d13r))
        quarters[2].append((z2[:, :128], z2[:, 128:]))
        quarters[3].append((d02r - d13i, d02i + d13r))
    for j in range(4):
        (r0, i0), (r1, i1) = quarters[j]
        data = jnp.concatenate(
            [jnp.concatenate([r0, r1], 1), jnp.concatenate([i0, i1], 1)], 0
        )
        out = dot3((w_ref[0, j], w_ref[1, j]), split(data))
        for part in range(2):
            for c in range(2):
                store(j, part, c, out[128 * part : 128 * part + 128, 128 * c : 128 * c + 128])


def store_into(flat_ref, step):
    def store(j, part, c, block):
        for k in range(CHANS):
            start = k * WIDE * 8 + j * 8 + part * 4 + c + 2 * step
            flat_ref[pl.ds(start, 8, stride=32), :] = block[8 * k : 8 * k + 8]

    return store


def add_edges(flat_ref):
    for k in range(CHANS):
        source = ((k + 1) % CHANS) * WIDE * 8
        flat_ref[pl.ds(k * WIDE * 8 + BINS * 8, 8), :] = flat_ref[pl.ds(source, 8), :]


def front0_kernel(chirp_ref, x_ref, w_ref, out_ref, rim_ref, pad_ref, kmat_ref):
    step = pl.program_id(0)

    @pl.when(step == 0)
    def _():
        fill_toeplitz(chirp_ref, pad_ref, kmat_ref)

    windows = []
    for c in range(2):
        windows.append(jnp.concatenate([x_ref[0, c], x_ref[1, c]], 1))
    rim_ref[...] = x_ref[:, :, :, :TILE]
    front_body(step, windows, kmat_ref, w_ref, store_into(out_ref, step))

    @pl.when(step == 1)
    def _():
        add_edges(out_ref)


def front1_kernel(chirp_ref, x_ref, h_ref, w_ref, out_ref, pad_ref, kmat_ref):
    step = pl.program_id(0)

    @pl.when(step == 0)
    def _():
        fill_toeplitz(chirp_ref, pad_ref, kmat_ref)

    windows = []
    for c in range(2):
        windows.append(jnp.concatenate([x_ref[0, c], h_ref[0, c], x_ref[1, c], h_ref[1, c]], 1))
    front_body(step, windows, kmat_ref, w_ref, store_into(out_ref, step))

    @pl.when(step == 1)
    def _():
        add_edges(out_ref)


def front_scratch():
    return [pltpu.VMEM((8, 2 * TILE), F32), pltpu.VMEM((2, 4 * TILE, 2 * TILE), BF16)]


def front0(chirp, echoes, w):
    return pl.pallas_call(
        front0_kernel,
        grid=(2,),
        in_specs=[
            pl.BlockSpec(chirp.shape, lambda i: (0, 0)),
            pl.BlockSpec((2, 2, PULSES, 2 * TILE), lambda i: (0, i, 0, 0)),
            pl.BlockSpec(w.shape, lambda i: (0, 0, 0, 0)),
        ],
        out_specs=[
            pl.BlockSpec((CHANS * WIDE * 8, TILE), lambda i: (0, 0)),
            pl.BlockSpec((2, 2, PULSES, TILE), lambda i: (0, i, 0, 0)),
        ],
        out_shape=[
            jax.ShapeDtypeStruct((CHANS * WIDE * 8, TILE), F32),
            jax.ShapeDtypeStruct((2, LOCAL, PULSES, TILE), F32),
        ],
        scratch_shapes=front_scratch(),
        compiler_params=params(),
        cost_estimate=cost(4e9, 12e6),
        name="front0",
    )(chirp, echoes, w)


def front1(chirp, echoes, rim, w):
    return pl.pallas_call(
        front1_kernel,
        grid=(2,),
        in_specs=[
            pl.BlockSpec(chirp.shape, lambda i: (0, 0)),
            pl.BlockSpec((2, 2, PULSES, TILE), lambda i: (0, i, 0, 1)),
            pl.BlockSpec((2, 2, PULSES, TILE), lambda i: (0, i, 0, 0)),
            pl.BlockSpec(w.shape, lambda i: (0, 0, 0, 0)),
        ],
        out_specs=pl.BlockSpec((CHANS * WIDE * 8, TILE), lambda i: (0, 0)),
        out_shape=jax.ShapeDtypeStruct((CHANS * WIDE * 8, TILE), F32),
        scratch_shapes=front_scratch(),
        compiler_params=params(),
        cost_estimate=cost(4e9, 8e6),
        name="front1",
    )(chirp, echoes, rim, w)


def unweave(blocks):
    pairs = blocks.reshape(CHANS // 2, 2, 8, TILE)
    even, odd = pairs[:, 0], pairs[:, 1]
    first = lax.broadcasted_iota(jnp.int32, even.shape, 1) < 4
    even_turned = pltpu.roll(even, 4, 1)
    odd_turned = pltpu.roll(odd, 4, 1)
    re = jnp.where(first, even, odd_turned).reshape(CHANS * LOCAL, TILE)
    im = jnp.where(first, even_turned, odd).reshape(CHANS * LOCAL, TILE)
    return re, im


def plant(place, blocks, store_spectra, high_ref, low_ref):
    re, im = unweave(blocks)
    rh, rl = split(re)
    ih, il = split(im)
    store_spectra(rh, ih)
    high_ref[0, place] = jnp.concatenate([rh, ih], 1)
    high_ref[1, place] = jnp.concatenate([ih, -rh], 1)
    low_ref[0, place] = jnp.concatenate([rl, il], 1)
    low_ref[1, place] = jnp.concatenate([il, -rl], 1)


def bin_gram(place, high_ref, low_ref):
    def rows(ref, kind):
        return ref[kind, pl.ds(place, 2)].reshape(128, 2 * TILE)

    ah, al = rows(high_ref, 0), rows(low_ref, 0)
    bh = jnp.concatenate([ah, rows(high_ref, 1)], 0)
    bl = jnp.concatenate([al, rows(low_ref, 1)], 0)
    both = dot3((ah, al), (bh, bl), ((1,), (1,)))
    row = lax.broadcasted_iota(jnp.int32, (128, 128), 0)
    column = lax.broadcasted_iota(jnp.int32, (128, 128), 1)
    return jnp.where(row <= column, both[:, :128], both[:, 128:])


def gram_scratch(count):
    return [pltpu.VMEM((2, count + 1, 64, 2 * TILE), BF16)] * 2


def plant_all(r_ref, edge_ref, spectra_ref, high_ref, low_ref):
    for b in range(GROUP):

        def store(rh, ih, b=b):
            spectra_ref[0, b] = rh
            spectra_ref[1, b] = ih

        plant(b, r_ref[:, b], store, high_ref, low_ref)
    plant(GROUP, edge_ref[:, 0], lambda rh, ih: None, high_ref, low_ref)


def gram0_kernel(mask_ref, r_ref, edge_ref, sums_ref, spectra_ref, high_ref, low_ref):
    first = pl.program_id(0) * GROUP
    plant_all(r_ref, edge_ref, spectra_ref, high_ref, low_ref)
    for b in range(GROUP):
        weight = mask_ref[0, first + b].astype(F32)
        sums_ref[b] = bin_gram(b, high_ref, low_ref) * weight


def gram0(mask, received):
    return pl.pallas_call(
        gram0_kernel,
        grid=(BINS // GROUP,),
        in_specs=[
            SMEM,
            pl.BlockSpec((CHANS, GROUP, 8, TILE), lambda i: (0, i, 0, 0)),
            pl.BlockSpec((CHANS, 1, 8, TILE), lambda i: (0, GROUP * (i + 1), 0, 0)),
        ],
        out_specs=[
            pl.BlockSpec((GROUP, 128, 128), lambda i: (i, 0, 0)),
            pl.BlockSpec((2, GROUP, 64, TILE), lambda i: (0, i, 0, 0)),
        ],
        out_shape=[
            jax.ShapeDtypeStruct((BINS, 128, 128), F32),
            jax.ShapeDtypeStruct((2, BINS, 64, 2 * TILE), BF16),
        ],
        scratch_shapes=gram_scratch(GROUP),
        compiler_params=params(20),
        cost_estimate=cost(2e9, 6e6),
        name="gram0",
    )(mask, received, received)


def gram1_kernel(other, spot_ref, mask_ref, r_ref, edge_ref, sums_ref, _, out_ref, spectra_ref, high_ref, low_ref):
    core = spot_ref[1]
    half = BINS // GROUP // 2
    first = ((1 - core if other else core) * half + pl.program_id(0)) * GROUP
    plant_all(r_ref, edge_ref, spectra_ref, high_ref, low_ref)
    for b in range(GROUP):
        weight = mask_ref[1, first + b].astype(F32)
        out_ref[b] = sums_ref[b] + bin_gram(b, high_ref, low_ref) * weight


def gram1(other, spot, mask, received, sums, spectra, name):
    half = BINS // GROUP // 2

    def at(i, spot):
        return (1 - spot[1] if other else spot[1]) * half + i

    return pl.pallas_call(
        functools.partial(gram1_kernel, other),
        grid_spec=pltpu.PrefetchScalarGridSpec(
            num_scalar_prefetch=1,
            grid=(half,),
            in_specs=[
                SMEM,
                pl.BlockSpec((CHANS, GROUP, 8, TILE), lambda i, spot: (0, at(i, spot), 0, 0)),
                pl.BlockSpec((CHANS, 1, 8, TILE), lambda i, spot: (0, GROUP * (at(i, spot) + 1), 0, 0)),
                pl.BlockSpec((GROUP, 128, 128), lambda i, spot: (at(i, spot), 0, 0)),
                ANY,
            ],
            out_specs=[
                pl.BlockSpec((GROUP, 128, 128), lambda i, spot: (i, 0, 0)),
                pl.BlockSpec((2, GROUP, 64, TILE), lambda i, spot: (0, at(i, spot), 0, 1)),
            ],
            scratch_shapes=gram_scratch(GROUP),
        ),
        out_shape=[
            jax.ShapeDtypeStruct((BINS // 2, 128, 128), F32),
            jax.ShapeDtypeStruct(spectra.shape, spectra.dtype),
        ],
        input_output_aliases={5: 1},
        compiler_params=params(20),
        cost_estimate=cost(2e9, 6e6),
        name=name,
    )(spot, mask, received, received, sums, spectra)


def core_sum_kernel(share, spot_ref, keep_ref, got_ref, *outs):
    for k, out_ref in enumerate(outs):
        base = lax.rem(spot_ref[0] + k, 4) * share
        out_ref[...] = keep_ref[pl.ds(base, share)] + got_ref[pl.ds(base, share)]


def core_sum(spot, keep, got):
    share = keep.shape[0] // 4
    return pl.pallas_call(
        functools.partial(core_sum_kernel, share),
        in_specs=[SMEM, VMEM, VMEM],
        out_specs=[VMEM] * 4,
        out_shape=[jax.ShapeDtypeStruct((share, 128, 128), F32)] * 4,
        compiler_params=params(16),
        cost_estimate=cost(1e6, 1e5),
        name="core_sum",
    )(spot, keep, got)


def spread(value):
    return jnp.broadcast_to(value, (8, 128))


def minus(value, left, right):
    re, im = value
    lr, li = left
    rr, ri = right
    return re - (lr * rr - li * ri), im - (lr * ri + li * rr)


def conj(value):
    return value[0], -value[1]


def four_columns(groups, i, place, store_row, last):
    columns = [
        [(spread(re[:, place + v : place + v + 1]), spread(im[:, place + v : place + v + 1])) for re, im in groups]
        for v in range(4)
    ]
    g, r = divmod(i, 8)
    corner = {}
    for u in range(4):
        for v in range(u, 4):
            re, im = columns[v][g]
            corner[u, v] = spread(re[r + u : r + u + 1]), spread(im[r + u : r + u + 1])
    re, im = groups[g]
    rows = [(spread(re[r + u : r + u + 1]), spread(im[r + u : r + u + 1])) for u in range(4)]
    inverses, upper = [], {}
    for t in range(4):
        inverse = lax.rsqrt(corner[t, t][0])
        inverses.append(inverse)
        for v in range(t + 1, 4):
            upper[t, v] = corner[t, v][0] * inverse, corner[t, v][1] * inverse
        for u in range(t + 1, 4):
            for v in range(u, 4):
                corner[u, v] = minus(corner[u, v], conj(upper[t, u]), upper[t, v])
    found = []
    for t in range(4):
        value = rows[t]
        for u in range(t):
            value = minus(value, conj(upper[u, t]), found[u])
        found.append((value[0] * inverses[t], value[1] * inverses[t]))
        store_row(place + t, found[t][0][0:1], found[t][1][0:1])
    if last:
        return groups
    later = []
    for g, value in enumerate(groups):
        if 8 * g + 8 > i + 4:
            scaled = []
            for t in range(4):
                column = columns[t][g]
                for u in range(t):
                    column = minus(column, scaled[u], upper[u, t])
                scaled.append((column[0] * inverses[t], column[1] * inverses[t]))
            for t in range(4):
                value = minus(value, scaled[t], found[t])
        later.append(value)
    return later


def factor_strips(offsets, count, gre_ref, gim_ref, fre_ref, fim_ref):
    base = offsets[0]
    for offset in offsets:
        strips = []
        for n in range(count):
            here = slice(offset - base, offset - base + STRIP)
            re, im = gre_ref[n, here], gim_ref[n, here]
            if offset:
                fr, fi = fre_ref[n, :offset], fim_ref[n, :offset]
                lr, li = fr[:, offset : offset + STRIP], fi[:, offset : offset + STRIP]
                left = jnp.concatenate(
                    [jnp.concatenate([lr, -li], 1), jnp.concatenate([li, lr], 1)], 0
                )
                update = lax.dot_general(
                    left,
                    jnp.concatenate([fr, fi], 0),
                    dimension_numbers=(((0,), (0,)), ((), ())),
                    preferred_element_type=F32,
                    precision=lax.Precision.HIGHEST,
                )
                re = re - update[:STRIP]
                im = im - update[STRIP:]
            strips.append([(re[8 * g : 8 * g + 8], im[8 * g : 8 * g + 8]) for g in range(STRIP // 8)])
        for i in range(0, STRIP, 4):
            for n in range(count):

                def store_row(place, re, im, n=n):
                    fre_ref[n, place : place + 1] = re
                    fim_ref[n, place : place + 1] = im

                strips[n] = four_columns(strips[n], i, offset + i, store_row, i + 4 == STRIP)
        r = lax.broadcasted_iota(jnp.int32, (STRIP, 128), 0) + offset
        c = lax.broadcasted_iota(jnp.int32, (STRIP, 128), 1)
        for n in range(count):
            here = slice(offset, offset + STRIP)
            fre_ref[n, here] = jnp.where(c >= r, fre_ref[n, here], 0.0)
            fim_ref[n, here] = jnp.where(c > r, fim_ref[n, here], 0.0)


def iota64():
    shape = (64, 128)
    return lax.broadcasted_iota(jnp.int32, shape, 0), lax.broadcasted_iota(jnp.int32, shape, 1)


def flip_blocks(value):
    turned = value.T
    return jnp.concatenate([turned[:64], turned[64:]], 1)


def top_kernel(scaling, *refs):
    ins = refs[:4]
    right_ref, side_ref, gre_ref, gim_ref, fre_ref, fim_ref = refs[4:]
    count = right_ref.shape[0]
    r, c = iota64()
    for n in range(count):
        packed = ins[0][n]
        for more in ins[1:]:
            packed = packed + more[n]
        packed = packed * scaling
        upper = packed[:64]
        turned = packed[:, :64].T
        gre_ref[n] = jnp.where(r <= c, upper, turned)
        gim_ref[n] = jnp.where(r < c, -turned, jnp.where(r > c, upper, 0.0))
        side_ref[n] = packed[64:]
    factor_strips((0, STRIP), count, gre_ref, gim_ref, fre_ref, fim_ref)
    for n in range(count):
        re, im = fre_ref[n], fim_ref[n]
        right_ref[n] = jnp.where(c < 64, pltpu.roll(im, 64, 1), re)
        corner = jnp.where(r <= c, re, flip_blocks(im))
        side_ref[n] = jnp.where(c < 64, corner, side_ref[n])


def bottom_kernel(right_ref, side_ref, out_ref, gre_ref, gim_ref, fre_ref, fim_ref):
    count = right_ref.shape[0]
    r, c = iota64()
    for n in range(count):
        right, side = right_ref[n], side_ref[n]
        fre_ref[n, :64] = jnp.where(c < 64, 0.0, right)
        fim_ref[n, :64] = jnp.where(c < 64, 0.0, pltpu.roll(right, 64, 1))
        turned = flip_blocks(side)
        gre_ref[n] = jnp.where(r <= c - 64, side, turned)
        gim_ref[n] = jnp.where(r < c - 64, -turned, jnp.where(r > c - 64, side, 0.0))
    factor_strips((64, 64 + STRIP), count, gre_ref, gim_ref, fre_ref, fim_ref)
    for n in range(count):
        re, im = fre_ref[n, 64:], fim_ref[n, 64:]
        corner = jnp.where(r <= c - 64, re, flip_blocks(im))
        out_ref[n] = jnp.where(c < 64, side_ref[n], corner)


def factor_top(pieces, scaling):
    count = pieces[0].shape[0]
    piece = jax.ShapeDtypeStruct((count, 64, 128), F32)
    return pl.pallas_call(
        functools.partial(top_kernel, scaling),
        in_specs=[VMEM] * 4,
        out_specs=[VMEM] * 2,
        out_shape=[piece] * 2,
        scratch_shapes=[pltpu.VMEM((count, 64, 128), F32)] * 4,
        compiler_params=params(16),
        cost_estimate=cost(1e6, 1e5),
        name="factor_top",
    )(*pieces)


def factor_bottom(right, side):
    count = right.shape[0]
    return pl.pallas_call(
        bottom_kernel,
        in_specs=[VMEM] * 2,
        out_specs=VMEM,
        out_shape=jax.ShapeDtypeStruct((count, 64, 128), F32),
        scratch_shapes=[pltpu.VMEM((count, 64, 128), F32)] * 2 + [pltpu.VMEM((count, 128, 128), F32)] * 2,
        compiler_params=params(16),
        cost_estimate=cost(1e6, 1e5),
        name="factor_bottom",
    )(right, side)


def hold_kernel(*refs):
    pass


def hold(value, until):
    return pl.pallas_call(
        hold_kernel,
        in_specs=[ANY] * (1 + len(until)),
        out_specs=ANY,
        out_shape=jax.ShapeDtypeStruct(value.shape, value.dtype),
        input_output_aliases={0: 0},
        compiler_params=params(16),
        cost_estimate=cost(1e3, 1e3),
        name="hold",
    )(value, *until)


def unpack_kernel(share, spot_ref, *refs):
    rights, corners, out_ref, held_ref, sems = refs[:8], refs[8:16], refs[16], refs[17], refs[18]
    r, c = iota64()
    y, core = spot_ref[0], spot_ref[1]
    copies = []
    for k in range(8):
        steps, other = k % 4, k // 4
        owner = lax.rem(y + 4 - steps, 4)
        whose = core + other - 2 * core * other
        base = (whose * 4 + owner) * share
        for i in range(share):
            right, corner = rights[k][i], corners[k][i]
            turned = flip_blocks(corner)
            place = k * share + i
            held_ref[place, 0, 0:64] = jnp.where(c < 64, jnp.where(r <= c, corner, 0.0), right)
            held_ref[place, 1, 0:64] = jnp.where(
                c < 64, jnp.where(r < c, turned, 0.0), pltpu.roll(right, 64, 1)
            )
            held_ref[place, 0, 64:128] = jnp.where(r <= c - 64, corner, 0.0)
            held_ref[place, 1, 64:128] = jnp.where(r < c - 64, turned, 0.0)
        copy = pltpu.make_async_copy(
            held_ref.at[pl.ds(k * share, share)], out_ref.at[pl.ds(base, share)], sems.at[k]
        )
        copy.start()
        copies.append(copy)
    for copy in copies:
        copy.wait()


def unpack(spot, rights, corners):
    share = rights[0].shape[0]
    return pl.pallas_call(
        functools.partial(unpack_kernel, share),
        in_specs=[SMEM] + [VMEM] * 16,
        out_specs=ANY,
        out_shape=jax.ShapeDtypeStruct((BINS, 2, 128, 128), F32),
        scratch_shapes=[
            pltpu.VMEM((8 * share, 2, 128, 128), F32),
            pltpu.SemaphoreType.DMA((8,)),
        ],
        compiler_params=params(16),
        cost_estimate=cost(1e6, 1e5),
        name="unpack",
    )(spot, *rights, *corners)


def along_y(value, steps):
    return lax.ppermute(value, "range", [(i, (i + 2 * steps) % 8) for i in range(8)])


def other_core(value):
    return lax.ppermute(value, "range", [(i, i ^ 1) for i in range(8)])


def across(value):
    return lax.all_to_all(value, "chan", split_axis=0, concat_axis=0, tiled=True)


def gather_sums(spot, keep, send):
    got = other_core(send)
    own, *rest = core_sum(spot, keep, got)
    return [own] + [along_y(piece, k + 1) for k, piece in enumerate(rest)]


def share_factors(mine):
    found = [mine] + [along_y(mine, k) for k in (1, 2, 3)]
    return found + [other_core(piece) for piece in found]


def on_device(echoes, chirp, train_mask):
    w = jnp.asarray(doppler_matrices())
    mask = train_mask.T
    here = lax.axis_index("range").astype(jnp.int32)
    spot = jnp.stack([here >> 1, here & 1])
    scaling = 1.0 / (2 * TILE * lax.axis_size("range"))
    flat0, rim = front0(chirp, echoes, w)
    halo = lax.ppermute(rim, "range", [(i, i - 1) for i in range(1, 8)])
    got0 = across(flat0.reshape(CHANS, WIDE, 8, TILE))
    got1 = across(front1(chirp, echoes, halo, w).reshape(CHANS, WIDE, 8, TILE))
    sums0, spectra = gram0(mask, got0)
    send, spectra = gram1(True, spot, mask, got1, sums0, spectra, "gram1_send")
    keep, spectra = gram1(False, spot, mask, got1, sums0, spectra, "gram1_keep")
    right, side = factor_top(gather_sums(spot, keep, send), scaling)
    rights = share_factors(right)
    corners = share_factors(hold(factor_bottom(right, side), rights[1:4]))
    factors = unpack(spot, rights, corners)
    return spectra, factors


def solution(mesh):
    return jax.shard_map(
        on_device,
        mesh=mesh,
        in_specs=(P(None, "chan", None, "range"), P(), P("chan", "range")),
        out_specs=(P(None, "chan", None, "range"), P("chan", None, None, None)),
        check_vma=False,
    )
```
